32 devices in a mesh: gz: 8 (over z, x), gy: 4 (over y, core).
Axes of the slice: x: 2, y: 2, z: 4, core: 2. Of those that a mesh axis runs over, the one named last changes fastest.
Arguments:
- populations: float32 [19, 8, 128, 256], P(None, 'gz', 'gy'), may hold values from 0 to 0.5, as said below
- solid_fraction: float32 [8, 128, 256], P('gz', 'gy'), may hold values from 0 to 1
- labels: int32 [8, 128, 256], P('gz', 'gy'), may hold values from 0 to 4, as said below
Outputs:
- sensitivity: float32 [8, 128, 256], P('gz', 'gy')
- adjoint_populations: float32 [19, 8, 128, 256], P(None, 'gz', 'gy')
The draws below stay inside these ranges and needn't reach their ends.
Inputs may be any that keep to these rules, and one draw needn't show every extreme that they name: `populations`: each population is w_q times a factor between 0.7 and 1.3. labels 3 appear only in the first plane along the feeding direction and 4 only in the last, in voxels that are not solid.
All inputs are finite; a program needn't handle non-finite values.
Results may differ from the reference program's by a relative error of at most 0.00028.
Values sent between devices are 32-bit elements; how exact they have to be, the bound alone decides.
No kernel may reach another device: no remote copies, remote signals or barrier semaphores. Data moves between devices by JAX's collectives and lax.ppermute only.
A program may use at most 64 MiB of HBM per device.

```python
import jax
import jax.numpy as jnp
from jax import lax

X = 256
STEPS = 2
NZ = 8
NY = 128


def draw_populations(key, part):
    weights = jnp.array([1.0 / 3.0] + [1.0 / 18.0] * 6 + [1.0 / 36.0] * 12, jnp.float32).reshape(19, 1, 1, 1)
    shape = (19, NZ, NY, X)
    zpos = lax.broadcasted_iota(jnp.float32, shape, 1)
    amplitude = 0.1 + 0.2 * zpos / max(NZ - 1, 1)
    noise = jax.random.uniform(key, shape, jnp.float32, -1.0, 1.0)
    return weights * (1.0 + amplitude * noise)


def draw_labels(key, part):
    shape = (NZ, NY, X)
    draws = jax.random.randint(key, shape, 0, 20)
    base = jnp.where(draws < 9, 0, jnp.where(draws < 15, 1, 2))
    zpos = lax.broadcasted_iota(jnp.int32, shape, 0)
    marked = jnp.where((zpos == 0) & (base != 2), 3, base)
    marked = jnp.where((zpos == NZ - 1) & (base != 2), 4, marked)
    return marked.astype(jnp.int32)


def shard_levels(rng, dims, cuts, least, top_value):
    gain, own = 1.0, jax.random.fold_in(rng, 6)
    for position, blocks in cuts:
        steps = jnp.exp(jax.random.uniform(jax.random.fold_in(own, position), (blocks,), jnp.float32, least / len(cuts), top_value / len(cuts)))
        gain = gain * jnp.repeat(steps, dims[position] // blocks).reshape([-1 if axis == position else 1 for axis in range(len(dims))])
    return gain


def setup_inputs(seed: int = 0) -> dict:
    streams_of = jax.random.split(jax.random.key(seed), 4)
    return {
        "populations": draw_populations(jax.random.fold_in(streams_of[3], 71), 0),
        "solid_fraction": jnp.clip(1.0 * jax.random.uniform(streams_of[1], (NZ, NY, X), jnp.float32) ** shard_levels(streams_of[1], (NZ, NY, X), ((0, 8), (1, 4)), -0.2, 0.2), 0.0, 1.0),
        "labels": draw_labels(jax.random.fold_in(streams_of[3], 71), 0),
    }


OMEGA = 0.9
INLET_SPEED = 0.05

def velocity_table():
    velocities = [(0, 0, 0)]
    for axis in range(3):
        for sign in (1, -1):
            vector = [0, 0, 0]
            vector[axis] = sign
            velocities.append(tuple(vector))
    for first in range(3):
        for second in range(first + 1, 3):
            for sign_a in (1, -1):
                for sign_b in (1, -1):
                    vector = [0, 0, 0]
                    vector[first] = sign_a
                    vector[second] = sign_b
                    velocities.append(tuple(vector))
    weights = [1.0 / 3.0] + [1.0 / 18.0] * 6 + [1.0 / 36.0] * 12
    opposite = [velocities.index(tuple((-e for e in vector))) for vector in velocities]
    return (velocities, weights, opposite)

def equilibrium(density, vel_x, vel_y, vel_z):
    velocities, weights, opposite = velocity_table()
    rows = []
    speed = vel_x * vel_x + vel_y * vel_y + vel_z * vel_z
    for index in range(19):
        cx, cy, cz = velocities[index]
        along = cx * vel_x + cy * vel_y + cz * vel_z
        rows.append(weights[index] * density * (1.0 + 3.0 * along + 4.5 * along * along - 1.5 * speed))
    return jnp.stack(rows)

def moments(field):
    velocities, weights, opposite = velocity_table()
    density = lax.optimization_barrier(jnp.sum(field, axis=0))
    mom_x = sum((velocities[q][0] * field[q] for q in range(19) if velocities[q][0] != 0))
    mom_y = sum((velocities[q][1] * field[q] for q in range(19) if velocities[q][1] != 0))
    mom_z = sum((velocities[q][2] * field[q] for q in range(19) if velocities[q][2] != 0))
    return (density, mom_x, mom_y, mom_z)

def collide(field, s_eff, labels):
    velocities, weights, opposite = velocity_table()
    density, mom_x, mom_y, mom_z = moments(field)
    feq = equilibrium(density, mom_x / density, mom_y / density, mom_z / density)
    rate = jnp.where(labels == 4, jnp.ones_like(density), OMEGA * jnp.ones_like(density))
    relaxed = field - rate * (field - feq)
    flipped = jnp.stack([field[opposite[q]] for q in range(19)])
    mixed = (1.0 - s_eff) * relaxed + s_eff * flipped
    ones = jnp.ones_like(density)
    inlet = equilibrium(ones, 0.0 * ones, 0.0 * ones, INLET_SPEED * ones)
    return jnp.where(labels == 3, inlet, mixed)

def energy(field, s_eff):
    density, mom_x, mom_y, mom_z = moments(field)
    return jnp.sum((1.0 - s_eff) * (mom_x * mom_x + mom_y * mom_y + mom_z * mom_z) / density)

def stream(field):
    velocities, weights, opposite = velocity_table()
    rows = []
    for q in range(19):
        cx, cy, cz = velocities[q]
        rows.append(jnp.roll(field[q], (cz, cy, cx), axis=(0, 1, 2)))
    return jnp.stack(rows)

def reference(populations, solid_fraction, labels):

    def total_energy(start, fraction):
        s_eff = jnp.where(labels == 1, fraction, jnp.where(labels == 2, jnp.ones_like(fraction), jnp.zeros_like(fraction)))

        def advance(carry, unused):
            field, result = carry
            field = stream(collide(field, s_eff, labels))
            result = result + energy(field, s_eff)
            return ((field, result), None)
        advance = jax.checkpoint(advance)
        carry, unused = lax.scan(advance, (start, jnp.zeros((), start.dtype)), jnp.arange(STEPS, dtype=jnp.int32))
        return carry[1]
    value, grads = jax.value_and_grad(total_energy, argnums=(0, 1))(populations, solid_fraction)
    mean_energy = value / (STEPS * NZ * NY * X)
    return (grads[1] / mean_energy, grads[0] / mean_energy)
```

```python
import functools

import jax
import jax.numpy as jnp
from jax import lax
from jax.experimental import pallas as pl
from jax.experimental.pallas import tpu as pltpu
from jax.sharding import PartitionSpec as P

STEPS = 2
OMEGA = 0.9
INLET_SPEED = 0.05
HALO = 4


def velocity_table():
    velocities = [(0, 0, 0)]
    for axis in range(3):
        for sign in (1, -1):
            vector = [0, 0, 0]
            vector[axis] = sign
            velocities.append(tuple(vector))
    for first in range(3):
        for second in range(first + 1, 3):
            for sign_a in (1, -1):
                for sign_b in (1, -1):
                    vector = [0, 0, 0]
                    vector[first] = sign_a
                    vector[second] = sign_b
                    velocities.append(tuple(vector))
    weights = [1.0 / 3.0] + [1.0 / 18.0] * 6 + [1.0 / 36.0] * 12
    opposite = [velocities.index(tuple((-e for e in vector))) for vector in velocities]
    return (velocities, weights, opposite)


VEL, WEIGHT, OPP = velocity_table()
Q = len(VEL)
FLAT = [q for q in range(Q) if VEL[q][2] == 0]
RISE = [q for q in range(Q) if VEL[q][2] == 1]
FALL = [q for q in range(Q) if VEL[q][2] == -1]


def inlet_value(q):
    along = VEL[q][2] * INLET_SPEED
    return WEIGHT[q] * (1.0 + 3.0 * along + 4.5 * along * along - 1.5 * INLET_SPEED * INLET_SPEED)


def signed_sum(terms):
    total = None
    for sign, term in terms:
        if total is None:
            total = term if sign > 0 else -term
        else:
            total = total + term if sign > 0 else total - term
    return total


def first_moments(f):
    out = []
    for axis in range(3):
        out.append(signed_sum(sorted(((VEL[q][axis], f[q]) for q in range(Q) if VEL[q][axis]), key=lambda t: -t[0])))
    return out


def dot_c(q, vector):
    return signed_sum(sorted(((VEL[q][a], vector[a]) for a in range(3) if VEL[q][a]), key=lambda t: -t[0]))


def macroscopic(f):
    rho = functools.reduce(lambda a, b: a + b, f)
    mom = first_moments(f)
    inv = 1.0 / rho
    u = [m * inv for m in mom]
    speed = u[0] * u[0] + u[1] * u[1] + u[2] * u[2]
    return rho, u, speed


def collide(f, s, lab):
    rho, u, speed = macroscopic(f)
    rate = jnp.where(lab == 4.0, 1.0, OMEGA)
    inlet = lab == 3.0
    free = 1.0 - s
    keep = free * (1.0 - rate)
    gain = free * rate * rho
    base = 1.0 - 1.5 * speed
    post = [None] * Q
    for q in range(Q):
        o = OPP[q]
        if o < q:
            continue
        scaled = gain * WEIGHT[q]
        if q == 0:
            post[0] = (keep + s) * f[0] + scaled * base
            continue
        along = dot_c(q, u)
        even = scaled * (base + 4.5 * along * along)
        odd = scaled * (3.0 * along)
        post[q] = keep * f[q] + s * f[o] + (even + odd)
        post[o] = keep * f[o] + s * f[q] + (even - odd)
    return [jnp.where(inlet, inlet_value(q), post[q]) for q in range(Q)], rho, u, speed


def pull_back(lam, f, s, lab):
    rho, u, speed = macroscopic(f)
    rate = jnp.where(lab == 4.0, 1.0, OMEGA)
    inlet = lab == 3.0
    lam = [jnp.where(inlet, 0.0, v) for v in lam]
    wsum = [None] * Q
    s0 = WEIGHT[0] * lam[0]
    axis_sum = functools.reduce(lambda a, b: a + b, [lam[q] for q in range(1, 7)])
    diag_sum = functools.reduce(lambda a, b: a + b, [lam[q] for q in range(7, Q)])
    s0 = s0 + WEIGHT[1] * axis_sum + WEIGHT[7] * diag_sum
    s1, tens = [], {}
    for a in range(3):
        near = signed_sum(sorted(((VEL[q][a], lam[q]) for q in range(1, 7) if VEL[q][a]), key=lambda t: -t[0]))
        far = signed_sum(sorted(((VEL[q][a], lam[q]) for q in range(7, Q) if VEL[q][a]), key=lambda t: -t[0]))
        s1.append(WEIGHT[1] * near + WEIGHT[7] * far)
        near = functools.reduce(lambda x, y: x + y, [lam[q] for q in range(1, 7) if VEL[q][a]])
        far = functools.reduce(lambda x, y: x + y, [lam[q] for q in range(7, Q) if VEL[q][a]])
        tens[a, a] = WEIGHT[1] * near + WEIGHT[7] * far
    for a in range(3):
        for b in range(a + 1, 3):
            cross = signed_sum(sorted(((VEL[q][a] * VEL[q][b], lam[q]) for q in range(7, Q) if VEL[q][a] * VEL[q][b]), key=lambda t: -t[0]))
            tens[a, b] = tens[b, a] = WEIGHT[7] * cross
    tu = [tens[a, 0] * u[0] + tens[a, 1] * u[1] + tens[a, 2] * u[2] for a in range(3)]
    utu = tu[0] * u[0] + tu[1] * u[1] + tu[2] * u[2]
    free = 1.0 - s
    by_rho = s0 * (1.0 + 1.5 * speed) - 4.5 * utu
    by_mom = [3.0 * s1[a] + 9.0 * tu[a] - 3.0 * u[a] * s0 for a in range(3)]
    keep = free * (1.0 - rate)
    gain = free * rate
    g0 = gain * by_rho
    gm = [gain * by_mom[a] for a in range(3)]
    out = [None] * Q
    bounce = lam[0] * f[0]
    plain = lam[0] * f[0]
    for q in range(Q):
        o = OPP[q]
        if o < q:
            continue
        if q == 0:
            out[0] = (keep + s) * lam[0] + g0
            continue
        along = dot_c(q, gm)
        out[q] = keep * lam[q] + s * lam[o] + (g0 + along)
        out[o] = keep * lam[o] + s * lam[q] + (g0 - along)
        bounce = bounce + (lam[q] * f[o] + lam[o] * f[q])
        plain = plain + (lam[q] * f[q] + lam[o] * f[o])
    s1u = s1[0] * u[0] + s1[1] * u[1] + s1[2] * u[2]
    at_eq = rho * (s0 * (1.0 - 1.5 * speed) + 3.0 * s1u + 4.5 * utu)
    by_s = bounce - (1.0 - rate) * plain - rate * at_eq
    return out, by_s, rho, u, speed


def shifted(value, dx, dy):
    if dx:
        value = pltpu.roll(value, dx % value.shape[1], 1)
    if dy:
        value = pltpu.roll(value, dy % value.shape[0], 0)
    return value


def tiles(rows):
    return [pl.ds(8 * t, 8) for t in range(rows // 8)]


def kernel_one(pop, frac, lab, from_low, from_high, mid, up, down, field, post):
    own = pop.shape[1]
    rows = own + 2 * HALO
    field[:Q, own : own + HALO, :] = from_high[:Q]
    field[:Q, own + HALO : rows, :] = from_low[:Q]
    mid[9:11, own : own + HALO, :] = from_high[Q : Q + 2]
    mid[9:11, own + HALO : rows, :] = from_low[Q : Q + 2]
    for t in tiles(rows):
        if t.start < own:
            label = lab[t, :].astype(jnp.float32)
            s = frac[t, :]
            f = [pop[q, t, :] for q in range(Q)]
        else:
            label = mid[10, t, :]
            s = mid[9, t, :]
            f = [field[q, t, :] for q in range(Q)]
        s = jnp.where(label == 1.0, s, jnp.where(label == 2.0, 1.0, 0.0))
        mid[9, t, :] = s
        mid[10, t, :] = label
        out, _, _, _ = collide(f, s, label)
        for q in range(Q):
            post[q, t, :] = out[q]
    for ref, group in ((mid, FLAT), (up, RISE), (down, FALL)):
        for i, q in enumerate(group):
            ref[i] = shifted(post[q], VEL[q][0], VEL[q][1])


def gather(q, mid, below, above):
    if VEL[q][2] == 0:
        return mid, FLAT.index(q)
    if VEL[q][2] == 1:
        return below, RISE.index(q)
    return above, FALL.index(q)


def kernel_two(mid, below, above, mom, up, down, part, post):
    rows = mid.shape[1]
    own = rows - 2 * HALO
    total = None
    for t in tiles(rows):
        f = []
        for q in range(Q):
            ref, i = gather(q, mid, below, above)
            f.append(ref[i, t, :])
        s = mid[9, t, :]
        out, rho, u, speed = collide(f, s, mid[10, t, :])
        for q in range(Q):
            post[q, t, :] = out[q]
        if t.start < own:
            e = (1.0 - s) * (rho * speed)
            total = e if total is None else total + e
    part[...] = total
    for ref, group in ((mom, FLAT), (up, RISE), (down, FALL)):
        sums = [None, None, None]
        for q in group:
            cx, cy, _ = VEL[q]
            v = shifted(post[q], cx, cy)
            for k, sign in ((0, 1), (1, cx), (2, cy)):
                if sign:
                    if sums[k] is None:
                        sums[k] = v if sign > 0 else -v
                    else:
                        sums[k] = sums[k] + v if sign > 0 else sums[k] - v
        for k in range(3):
            ref[k] = sums[k]


def kernel_three(mom, below, above, mid, part, mine, up, down, kinetic, out):
    rows = mom.shape[1]
    own = rows - 2 * HALO
    total = part[...]
    for t in tiles(rows):
        rho = mom[0, t, :] + below[0, t, :] + above[0, t, :]
        inv = 1.0 / rho
        ux = (mom[1, t, :] + below[1, t, :] + above[1, t, :]) * inv
        uy = (mom[2, t, :] + below[2, t, :] + above[2, t, :]) * inv
        uz = (below[0, t, :] - above[0, t, :]) * inv
        speed = ux * ux + uy * uy + uz * uz
        free = 1.0 - mid[9, t, :]
        two = 2.0 * free
        ax, ay, az, b = two * ux, two * uy, two * uz, free * speed
        mine[0, t, :] = ax
        mine[1, t, :] = ay
        mine[2, t, :] = b
        down[0, t, :] = ax
        down[1, t, :] = ay
        down[2, t, :] = az - b
        up[0, t, :] = ax
        up[1, t, :] = ay
        up[2, t, :] = -az - b
        if t.start < own:
            k = rho * speed
            kinetic[t, :] = k
            total = total + free * k
    half = total.shape[1] // 2
    out[...] = total[:, :half] + total[:, half:]


def kernel_four(mid, below, above, mine, low, high, kinetic, flat, up, down, lam, adj):
    rows = mid.shape[1]
    own = rows - 2 * HALO
    for q in range(Q):
        cx, cy, cz = VEL[q]
        ref = {0: mine, 1: high, -1: low}[cz]
        value = ref[2]
        if cz == 0:
            value = -value
        if cx:
            value = value + ref[0] if cx > 0 else value - ref[0]
        if cy:
            value = value + ref[1] if cy > 0 else value - ref[1]
        lam[q] = shifted(value, -cx, -cy)
    for t in tiles(rows):
        f = []
        for q in range(Q):
            ref, i = gather(q, mid, below, above)
            f.append(ref[i, t, :])
        s = mid[9, t, :]
        out, by_s, rho, u, speed = pull_back([lam[q, t, :] for q in range(Q)], f, s, mid[10, t, :])
        free = 1.0 - s
        two = [2.0 * free * u[a] for a in range(3)]
        less = free * speed
        for q in range(Q):
            e = out[q] - less
            adj[q, t, :] = e + dot_c(q, two) if q else e
        if t.start < own:
            flat[9, t, :] = by_s - rho * speed - kinetic[t, :]
    for ref, group in ((flat, FLAT), (up, FALL), (down, RISE)):
        for i, q in enumerate(group):
            ref[i] = shifted(adj[q], -VEL[q][0], -VEL[q][1])[:own]


def kernel_five(cells, pop, frac, lab, flat, low, high, energy, sens, out):
    own = pop.shape[1]
    scale = cells / jnp.sum(energy[...], keepdims=True)
    scale = jnp.broadcast_to(scale, (8, pop.shape[2]))
    for t in tiles(own):
        label = lab[t, :].astype(jnp.float32)
        s = jnp.where(label == 1.0, frac[t, :], jnp.where(label == 2.0, 1.0, 0.0))
        lam = []
        for q in range(Q):
            ref, i = {0: (flat, FLAT), 1: (high, RISE), -1: (low, FALL)}[VEL[q][2]]
            lam.append(ref[i.index(q), t, :])
        grads, by_s, _, _, _ = pull_back(lam, [pop[q, t, :] for q in range(Q)], s, label)
        for q in range(Q):
            out[q, t, :] = grads[q] * scale
        sens[t, :] = jnp.where(label == 1.0, (by_s + flat[9, t, :]) * scale, 0.0)


def call(kernel, shapes, scratch, *args):
    return pl.pallas_call(
        kernel,
        out_shape=[jax.ShapeDtypeStruct(s, jnp.float32) for s in shapes],
        in_specs=[pl.BlockSpec(memory_space=pltpu.VMEM)] * len(args),
        out_specs=[pl.BlockSpec(memory_space=pltpu.VMEM)] * len(shapes),
        scratch_shapes=[pltpu.VMEM(s, jnp.float32) for s in scratch],
        compiler_params=pltpu.CompilerParams(vmem_limit_bytes=16 * 1024 * 1024),
    )(*args)


def passed_along(array, axis, by):
    count = lax.axis_size(axis)
    return lax.ppermute(array, axis, [(i, (i + by) % count) for i in range(count)])


def total_over(value, axes):
    for axis in axes:
        count = lax.axis_size(axis)
        if count & (count - 1):
            value = lax.psum(value, axis)
            continue
        step = 1
        while step < count:
            value = value + lax.ppermute(value, axis, [(i, i ^ step) for i in range(count)])
            step *= 2
    return value


def on_device(populations, solid_fraction, labels):
    _, _, own, wide = populations.shape
    rows = own + 2 * HALO
    pop = populations.reshape(Q, own, wide)
    frac = solid_fraction.reshape(own, wide)
    lab = labels.reshape(own, wide)

    def edge(cut):
        return jnp.concatenate([pop[:, cut], frac[None, cut], lab[None, cut].astype(jnp.float32)], axis=0)

    from_low = passed_along(edge(slice(own - HALO, own)), "gy", 1)
    from_high = passed_along(edge(slice(0, HALO)), "gy", -1)
    full = lambda n: (n, rows, wide)
    mid, up, down = call(
        kernel_one, [full(11), full(5), full(5)], [full(Q), full(Q)], pop, frac, lab, from_low, from_high
    )
    below, above = passed_along(up, "gz", 1), passed_along(down, "gz", -1)
    mom, up, down, part = call(
        kernel_two, [full(3), full(3), full(3), (8, wide)], [full(Q)], mid, below, above
    )
    low, high = passed_along(up, "gz", 1), passed_along(down, "gz", -1)
    mine, up, down, kinetic, energy = call(
        kernel_three, [full(3), full(3), full(3), (own, wide), (8, wide // 2)], [], mom, low, high, mid, part
    )
    energy = total_over(energy, ("gy", "gz"))
    low, high = passed_along(up, "gz", 1), passed_along(down, "gz", -1)
    less = lambda n: (n, own, wide)
    flat, up, down = call(
        kernel_four, [less(10), less(5), less(5)], [full(Q), full(Q)], mid, below, above, mine, low, high, kinetic
    )
    low, high = passed_along(up, "gz", 1), passed_along(down, "gz", -1)
    cells = float(STEPS * own * wide * populations.shape[1] * lax.axis_size("gz") * lax.axis_size("gy"))
    sens, out = call(
        functools.partial(kernel_five, cells), [(own, wide), less(Q)], [], pop, frac, lab, flat, low, high, energy
    )
    return sens.reshape(solid_fraction.shape), out.reshape(populations.shape)


def solution(mesh):
    in_specs = (P(None, "gz", "gy", None), P("gz", "gy", None), P("gz", "gy", None))
    out_specs = (P("gz", "gy", None), P(None, "gz", "gy", None))
    return jax.shard_map(on_device, mesh=mesh, in_specs=in_specs, out_specs=out_specs, check_vma=False)
```

```python
import functools

import jax
import jax.numpy as jnp
from jax import lax
from jax.experimental import pallas as pl
from jax.experimental.pallas import tpu as pltpu
from jax.sharding import PartitionSpec as P

STEPS = 2
OMEGA = 0.9
INLET_SPEED = 0.05
HALO = 4
WORK = 20_000_000
EARLY = 2
ALPHA, BETA = 1, 0


def velocity_table():
    velocities = [(0, 0, 0)]
    for axis in range(3):
        for sign in (1, -1):
            vector = [0, 0, 0]
            vector[axis] = sign
            velocities.append(tuple(vector))
    for first in range(3):
        for second in range(first + 1, 3):
            for sign_a in (1, -1):
                for sign_b in (1, -1):
                    vector = [0, 0, 0]
                    vector[first] = sign_a
                    vector[second] = sign_b
                    velocities.append(tuple(vector))
    weights = [1.0 / 3.0] + [1.0 / 18.0] * 6 + [1.0 / 36.0] * 12
    opposite = [velocities.index(tuple((-e for e in vector))) for vector in velocities]
    return (velocities, weights, opposite)


VEL, WEIGHT, OPP = velocity_table()
Q = len(VEL)
FLAT = [q for q in range(Q) if VEL[q][2] == 0]
RISE = [q for q in range(Q) if VEL[q][2] == 1]
FALL = [q for q in range(Q) if VEL[q][2] == -1]


def inlet_value(q):
    along = VEL[q][2] * INLET_SPEED
    return WEIGHT[q] * (1.0 + 3.0 * along + 4.5 * along * along - 1.5 * INLET_SPEED * INLET_SPEED)


def signed_sum(terms):
    total = None
    for sign, term in terms:
        if total is None:
            total = term if sign > 0 else -term
        else:
            total = total + term if sign > 0 else total - term
    return total


def first_moments(f):
    out = []
    for axis in range(3):
        out.append(signed_sum(sorted(((VEL[q][axis], f[q]) for q in range(Q) if VEL[q][axis]), key=lambda t: -t[0])))
    return out


def dot_c(q, vector):
    return signed_sum(sorted(((VEL[q][a], vector[a]) for a in range(3) if VEL[q][a]), key=lambda t: -t[0]))


def macroscopic(f):
    rho = functools.reduce(lambda a, b: a + b, f)
    mom = first_moments(f)
    inv = 1.0 / rho
    u = [m * inv for m in mom]
    speed = u[0] * u[0] + u[1] * u[1] + u[2] * u[2]
    return rho, u, speed


def collide(f, s, lab):
    rho, u, speed = macroscopic(f)
    rate = jnp.where(lab == 4.0, 1.0, OMEGA)
    inlet = lab == 3.0
    free = 1.0 - s
    keep = free * (1.0 - rate)
    gain = free * rate * rho
    base = 1.0 - 1.5 * speed
    post = [None] * Q
    for q in range(Q):
        o = OPP[q]
        if o < q:
            continue
        scaled = gain * WEIGHT[q]
        if q == 0:
            post[0] = (keep + s) * f[0] + scaled * base
            continue
        along = dot_c(q, u)
        even = scaled * (base + 4.5 * along * along)
        odd = scaled * (3.0 * along)
        post[q] = keep * f[q] + s * f[o] + (even + odd)
        post[o] = keep * f[o] + s * f[q] + (even - odd)
    return [jnp.where(inlet, inlet_value(q), post[q]) for q in range(Q)], rho, u, speed


def pull_back(lam, f, s, lab):
    rho, u, speed = macroscopic(f)
    rate = jnp.where(lab == 4.0, 1.0, OMEGA)
    inlet = lab == 3.0
    lam = [jnp.where(inlet, 0.0, v) for v in lam]
    wsum = [None] * Q
    s0 = WEIGHT[0] * lam[0]
    axis_sum = functools.reduce(lambda a, b: a + b, [lam[q] for q in range(1, 7)])
    diag_sum = functools.reduce(lambda a, b: a + b, [lam[q] for q in range(7, Q)])
    s0 = s0 + WEIGHT[1] * axis_sum + WEIGHT[7] * diag_sum
    s1, tens = [], {}
    for a in range(3):
        near = signed_sum(sorted(((VEL[q][a], lam[q]) for q in range(1, 7) if VEL[q][a]), key=lambda t: -t[0]))
        far = signed_sum(sorted(((VEL[q][a], lam[q]) for q in range(7, Q) if VEL[q][a]), key=lambda t: -t[0]))
        s1.append(WEIGHT[1] * near + WEIGHT[7] * far)
        near = functools.reduce(lambda x, y: x + y, [lam[q] for q in range(1, 7) if VEL[q][a]])
        far = functools.reduce(lambda x, y: x + y, [lam[q] for q in range(7, Q) if VEL[q][a]])
        tens[a, a] = WEIGHT[1] * near + WEIGHT[7] * far
    for a in range(3):
        for b in range(a + 1, 3):
            cross = signed_sum(sorted(((VEL[q][a] * VEL[q][b], lam[q]) for q in range(7, Q) if VEL[q][a] * VEL[q][b]), key=lambda t: -t[0]))
            tens[a, b] = tens[b, a] = WEIGHT[7] * cross
    tu = [tens[a, 0] * u[0] + tens[a, 1] * u[1] + tens[a, 2] * u[2] for a in range(3)]
    utu = tu[0] * u[0] + tu[1] * u[1] + tu[2] * u[2]
    free = 1.0 - s
    by_rho = s0 * (1.0 + 1.5 * speed) - 4.5 * utu
    by_mom = [3.0 * s1[a] + 9.0 * tu[a] - 3.0 * u[a] * s0 for a in range(3)]
    keep = free * (1.0 - rate)
    gain = free * rate
    g0 = gain * by_rho
    gm = [gain * by_mom[a] for a in range(3)]
    out = [None] * Q
    bounce = lam[0] * f[0]
    plain = lam[0] * f[0]
    for q in range(Q):
        o = OPP[q]
        if o < q:
            continue
        if q == 0:
            out[0] = (keep + s) * lam[0] + g0
            continue
        along = dot_c(q, gm)
        out[q] = keep * lam[q] + s * lam[o] + (g0 + along)
        out[o] = keep * lam[o] + s * lam[q] + (g0 - along)
        bounce = bounce + (lam[q] * f[o] + lam[o] * f[q])
        plain = plain + (lam[q] * f[q] + lam[o] * f[o])
    s1u = s1[0] * u[0] + s1[1] * u[1] + s1[2] * u[2]
    at_eq = rho * (s0 * (1.0 - 1.5 * speed) + 3.0 * s1u + 4.5 * utu)
    by_s = bounce - (1.0 - rate) * plain - rate * at_eq
    return out, by_s, rho, u, speed


def shifted(value, dx, dy):
    if dx:
        value = pltpu.roll(value, dx % value.shape[1], 1)
    if dy:
        value = pltpu.roll(value, dy % value.shape[0], 0)
    return value


def tiles(rows):
    return [pl.ds(8 * t, 8) for t in range(rows // 8)]


def pick(odd, first, second):
    return jnp.where(odd, second, first)


def write_pair(odd, to_pair, to_other, rising, falling):
    to_pair[...] = pick(odd, rising, falling)
    to_other[...] = pick(odd, falling, rising)


def kernel_pack(odd_y, pop, cell, edge_pair, edge_other):
    own = pop.shape[1]
    oy = odd_y[0] == 1
    for i in range(Q + 2):
        ref = pop.at[i] if i < Q else cell.at[i - Q]
        write_pair(oy, edge_pair.at[i], edge_other.at[i], ref[own - HALO : own, :], ref[0:HALO, :])


def kernel_one(odd_z, odd_y, pop, cell, edge_pair, edge_other, mid, pair, other, tile, post):
    own = pop.shape[1]
    rows = mid.shape[1]
    oz, oy = odd_z[0] == 1, odd_y[0] == 1
    for i in range(Q + 2):
        a, b = edge_pair[i], edge_other[i]
        tile[i, :HALO, :] = pick(oy, a, b)
        tile[i, HALO:, :] = pick(oy, b, a)
    for t in tiles(rows):
        if t.start < own:
            f = [pop[q, t, :] for q in range(Q)]
            s, label = cell[0, t, :], cell[1, t, :]
        else:
            f = [tile[q] for q in range(Q)]
            s, label = tile[Q], tile[Q + 1]
        mid[len(FLAT), t, :] = s
        mid[len(FLAT) + 1, t, :] = label
        out, _, _, _ = collide(f, s, label)
        for q in range(Q):
            post[q, t, :] = out[q]
    moved = lambda q: shifted(post[q], VEL[q][0], VEL[q][1])
    for i, q in enumerate(FLAT):
        mid[i] = moved(q)
    for i in range(len(RISE)):
        write_pair(oz, pair.at[i], other.at[i], moved(RISE[i]), moved(FALL[i]))


def kernel_two(odd_p, mid, pair, other, field, mom, to_pair, to_other, part, post):
    rows = field.shape[1]
    own = rows - 2 * HALO
    odd = odd_p[0] == 1
    for q in range(Q):
        cz = VEL[q][2]
        if cz == 0:
            value = mid[FLAT.index(q)]
        elif cz == 1:
            i = RISE.index(q)
            value = pick(odd, other[i], pair[i])
        else:
            i = FALL.index(q)
            value = pick(odd, pair[i], other[i])
        field[q] = value
    for i in (0, 1):
        field[Q + i] = mid[len(FLAT) + i]
    total = None
    for t in tiles(rows):
        s = field[Q, t, :]
        out, rho, u, speed = collide([field[q, t, :] for q in range(Q)], s, field[Q + 1, t, :])
        for q in range(Q):
            post[q, t, :] = out[q]
        if t.start < own:
            e = (1.0 - s) * (rho * speed)
            total = e if total is None else total + e
    part[...] = total
    results = []
    for group in (FLAT, RISE, FALL):
        sums = [None, None, None]
        for q in group:
            cx, cy, _ = VEL[q]
            v = shifted(post[q], cx, cy)
            for k, sign in ((0, 1), (1, cx), (2, cy)):
                if sign:
                    if sums[k] is None:
                        sums[k] = v if sign > 0 else -v
                    else:
                        sums[k] = sums[k] + v if sign > 0 else sums[k] - v
        results.append(sums)
    for k in range(3):
        mom[k] = results[0][k]
        write_pair(odd, to_pair.at[k], to_other.at[k], results[1][k], results[2][k])


def kernel_three(odd_p, mom, pair, other, field, part, mine, to_pair, to_other, kinetic, out):
    rows = mom.shape[1]
    own = rows - 2 * HALO
    odd = odd_p[0] == 1
    total = part[...]
    for t in tiles(rows):
        below = [pick(odd, other[k, t, :], pair[k, t, :]) for k in range(3)]
        above = [pick(odd, pair[k, t, :], other[k, t, :]) for k in range(3)]
        rho = mom[0, t, :] + below[0] + above[0]
        inv = 1.0 / rho
        ux = (mom[1, t, :] + below[1] + above[1]) * inv
        uy = (mom[2, t, :] + below[2] + above[2]) * inv
        uz = (below[0] - above[0]) * inv
        speed = ux * ux + uy * uy + uz * uz
        free = 1.0 - field[Q, t, :]
        two = 2.0 * free
        ax, ay, az, b = two * ux, two * uy, two * uz, free * speed
        mine[0, t, :] = ax
        mine[1, t, :] = ay
        mine[2, t, :] = b
        to_pair[0, t, :] = ax
        to_pair[1, t, :] = ay
        to_other[0, t, :] = ax
        to_other[1, t, :] = ay
        write_pair(odd, to_pair.at[2, t, :], to_other.at[2, t, :], -az - b, az - b)
        if t.start < own:
            k = rho * speed
            kinetic[t, :] = k
            total = total + free * k
    half = total.shape[1] // 2
    out[...] = total[:, :half] + total[:, half:]


def kernel_four(odd_p, field, mine, pair, other, kinetic, energy, flat, to_pair, to_other, lam, adj):
    rows = field.shape[1]
    own = rows - 2 * HALO
    odd = odd_p[0] == 1
    low = [pick(odd, other[k], pair[k]) for k in range(3)]
    high = [pick(odd, pair[k], other[k]) for k in range(3)]
    for q in range(Q):
        cx, cy, cz = VEL[q]
        ref = {0: mine, 1: high, -1: low}[cz]
        value = ref[2]
        if cz == 0:
            value = -value
        if cx:
            value = value + ref[0] if cx > 0 else value - ref[0]
        if cy:
            value = value + ref[1] if cy > 0 else value - ref[1]
        lam[q] = shifted(value, -cx, -cy)
    for t in tiles(rows):
        s = field[Q, t, :]
        out, by_s, rho, u, speed = pull_back(
            [lam[q, t, :] for q in range(Q)], [field[q, t, :] for q in range(Q)], s, field[Q + 1, t, :]
        )
        free = 1.0 - s
        two = [2.0 * free * u[a] for a in range(3)]
        less = free * speed
        for q in range(Q):
            e = out[q] - less
            adj[q, t, :] = e + dot_c(q, two) if q else e
        if t.start < own:
            flat[len(FLAT), t, :] = by_s - rho * speed - kinetic[t, :]

    def pulled(q):
        return shifted(adj[q], -VEL[q][0], -VEL[q][1])[:own]

    for i, q in enumerate(FLAT):
        flat[i] = pulled(q)
    for i in range(len(RISE)):
        write_pair(odd, to_pair.at[i], to_other.at[i], pulled(FALL[i]), pulled(RISE[i]))


def kernel_five(cells, odd_z, pop, cell, flat, pair, other, energy, sens_h, out_h, sens, out, sems):
    own = pop.shape[1]
    odd = odd_z[0] == 1
    copies = []
    scale = cells / jnp.sum(energy[...], keepdims=True)
    scale = jnp.broadcast_to(scale, (8, pop.shape[2]))
    for t in tiles(own):
        s, label = cell[0, t, :], cell[1, t, :]
        lam = []
        for q in range(Q):
            if VEL[q][2] == 0:
                lam.append(flat[FLAT.index(q), t, :])
            elif VEL[q][2] == 1:
                i = RISE.index(q)
                lam.append(pick(odd, pair[i, t, :], other[i, t, :]))
            else:
                i = FALL.index(q)
                lam.append(pick(odd, other[i, t, :], pair[i, t, :]))
        grads, by_s, _, _, _ = pull_back(lam, [pop[q, t, :] for q in range(Q)], s, label)
        for q in range(Q):
            out[q, t, :] = grads[q] * scale
        sens[t, :] = jnp.where(label == 1.0, (by_s + flat[len(FLAT), t, :]) * scale, 0.0)
        n = t.start // 8
        copies.append(pltpu.make_async_copy(out.at[:, t, :], out_h.at[:, t, :], sems.at[n]))
        copies[-1].start()
    copies.append(pltpu.make_async_copy(sens, sens_h, sems.at[own // 8]))
    copies[-1].start()
    for c in copies:
        c.wait()


def call(kernel, shapes, scratch, flags, *args, hbm_out=False, sems=0, work=0):
    fast = pl.BlockSpec(memory_space=pltpu.VMEM)
    slow = pl.BlockSpec(memory_space=pltpu.HBM)
    return pl.pallas_call(
        kernel,
        out_shape=[jax.ShapeDtypeStruct(s, jnp.float32) for s in shapes],
        in_specs=[pl.BlockSpec(memory_space=pltpu.SMEM)] * len(flags)
        + [fast] * len(args),
        out_specs=[slow if hbm_out else fast] * len(shapes),
        scratch_shapes=[pltpu.VMEM(s, jnp.float32) for s in scratch]
        + ([pltpu.SemaphoreType.DMA((sems,))] if sems else []),
        compiler_params=pltpu.CompilerParams(vmem_limit_bytes=16 * 1024 * 1024),
        cost_estimate=pl.CostEstimate(flops=0, transcendentals=0, bytes_accessed=work) if work else None,
    )(*flags, *args)


def doubled(value, steps):
    for axis, step in steps:
        count = lax.axis_size(axis)
        value = value + lax.ppermute(value, axis, [(i, i ^ step) for i in range(count)])
    return value


def doublings(count):
    return [1 << b for b in range(count.bit_length() - 1)]


class Layout:
    def __init__(self, planes, chunks):
        self.planes, self.chunks = planes, chunks
        self.bricks = [(p, k) for p in range(planes) for k in range(chunks)]
        self.swapped = planes % 2 == 0 and chunks % 2 == 0

    def start(self, p, k):
        return (p % self.planes) * self.chunks + k % self.chunks

    def home(self, p, k):
        p, k = p % self.planes, k % self.chunks
        if not self.swapped:
            return self.start(p, k)
        return self.start(p - p % 2 + (k + ALPHA) % 2, k - k % 2 + (p + BETA) % 2)

    def moves(self, source, target):
        side = lambda p: 1 - 2 * (p % 2)
        still = [(source(p, k), target(p, k)) for p, k in self.bricks]
        pair = [(source(p, k), target(p + side(p), k)) for p, k in self.bricks]
        other = [(source(p, k), target(p - side(p), k)) for p, k in self.bricks]
        return still, pair, other


def on_device(populations, solid_fraction, labels):
    _, _, own, wide = populations.shape
    rows = own + 2 * HALO
    axes = ("gz", "gy")
    planes, chunks = lax.axis_size("gz"), lax.axis_size("gy")
    layout = Layout(planes, chunks)
    flag = lambda axis: (lax.axis_index(axis) % 2).astype(jnp.int32).reshape(1)
    odd_z, odd_y = flag("gz"), flag("gy")
    odd_p = (odd_y + BETA) % 2 if layout.swapped else odd_z
    pop = populations.reshape(Q, own, wide)
    frac = solid_fraction.reshape(own, wide)
    lab = labels.reshape(own, wide)
    whole = lambda n: (n, rows, wide)
    less = lambda n: (n, own, wide)
    edge = lambda n: (n, 2 * HALO, wide)

    mixed = jnp.where(lab == 1, frac, jnp.where(lab == 2, jnp.float32(1.0), jnp.float32(0.0)))
    cell = jnp.stack([mixed, lab.astype(jnp.float32)])
    edge_a, edge_b = call(kernel_pack, [(Q + 2, HALO, wide)] * 2, [], [odd_y], pop, cell)
    side = lambda k: 1 - 2 * (k % 2)
    edge_a = lax.ppermute(edge_a, "gy", [(k, (k + side(k)) % chunks) for k in range(chunks)])
    edge_b = lax.ppermute(edge_b, "gy", [(k, (k - side(k)) % chunks) for k in range(chunks)])
    mid, pair, other = call(
        kernel_one,
        [whole(11), whole(5), whole(5)],
        [edge(Q + 2), whole(Q)],
        [odd_z, odd_y],
        pop,
        cell,
        edge_a,
        edge_b,
    )
    still_p, pair_p, other_p = layout.moves(layout.start, layout.home)
    mid = lax.ppermute(mid, axes, still_p)
    other = lax.ppermute(other, axes, other_p)
    pair = lax.ppermute(pair, axes, pair_p)
    field, mom, pair, other, part = call(
        kernel_two,
        [whole(Q + 2), whole(3), whole(3), whole(3), (8, wide)],
        [whole(Q)],
        [odd_p],
        mid,
        pair,
        other,
    )
    _, pair_p, other_p = layout.moves(layout.home, layout.home)
    other = lax.ppermute(other, axes, other_p)
    pair = lax.ppermute(pair, axes, pair_p)
    mine, pair, other, kinetic, energy = call(
        kernel_three,
        [whole(3), whole(3), whole(3), (own, wide), (8, wide // 2)],
        [],
        [odd_p],
        mom,
        pair,
        other,
        field,
        part,
    )
    other = lax.ppermute(other, axes, other_p)
    pair = lax.ppermute(pair, axes, pair_p)
    steps = [("gy", d) for d in doublings(chunks)] + [("gz", d) for d in doublings(planes)]
    steps.sort(key=lambda t: t[1])
    energy = doubled(energy, steps[:EARLY])
    flat, pair, other = call(
        kernel_four,
        [less(10), less(5), less(5)],
        [whole(Q), whole(Q)],
        [odd_p],
        field,
        mine,
        pair,
        other,
        kinetic,
        energy,
        work=WORK,
    )
    still_p, pair_p, other_p = layout.moves(layout.home, layout.start)
    energy = doubled(energy, steps[EARLY:])
    pair = lax.ppermute(pair, axes, pair_p)
    other = lax.ppermute(other, axes, other_p)
    flat = lax.ppermute(flat, axes, still_p)
    cells = float(STEPS * own * wide * populations.shape[1] * planes * chunks)
    sens, out = call(
        functools.partial(kernel_five, cells),
        [(own, wide), less(Q)],
        [(own, wide), less(Q)],
        [odd_z],
        pop,
        cell,
        flat,
        pair,
        other,
        energy,
        hbm_out=True,
        sems=own // 8 + 1,
    )
    return sens.reshape(solid_fraction.shape), out.reshape(populations.shape)


def solution(mesh):
    in_specs = (P(None, "gz", "gy", None), P("gz", "gy", None), P("gz", "gy", None))
    out_specs = (P("gz", "gy", None), P(None, "gz", "gy", None))
    return jax.shard_map(on_device, mesh=mesh, in_specs=in_specs, out_specs=out_specs, check_vma=False)
```

```python
import functools

import jax
import jax.numpy as jnp
from jax import lax
from jax.experimental import pallas as pl
from jax.experimental.pallas import tpu as pltpu
from jax.sharding import PartitionSpec as P

STEPS = 2
OMEGA = 0.9
INLET_SPEED = 0.05
HALO = 4
ALPHA, BETA = 1, 0


def velocity_table():
    velocities = [(0, 0, 0)]
    for axis in range(3):
        for sign in (1, -1):
            vector = [0, 0, 0]
            vector[axis] = sign
            velocities.append(tuple(vector))
    for first in range(3):
        for second in range(first + 1, 3):
            for sign_a in (1, -1):
                for sign_b in (1, -1):
                    vector = [0, 0, 0]
                    vector[first] = sign_a
                    vector[second] = sign_b
                    velocities.append(tuple(vector))
    weights = [1.0 / 3.0] + [1.0 / 18.0] * 6 + [1.0 / 36.0] * 12
    opposite = [velocities.index(tuple((-e for e in vector))) for vector in velocities]
    return (velocities, weights, opposite)


VEL, WEIGHT, OPP = velocity_table()
Q = len(VEL)
FLAT = [q for q in range(Q) if VEL[q][2] == 0]
RISE = [q for q in range(Q) if VEL[q][2] == 1]
FALL = [q for q in range(Q) if VEL[q][2] == -1]


def inlet_value(q):
    along = VEL[q][2] * INLET_SPEED
    return WEIGHT[q] * (1.0 + 3.0 * along + 4.5 * along * along - 1.5 * INLET_SPEED * INLET_SPEED)


def signed_sum(terms):
    total = None
    for sign, term in terms:
        if total is None:
            total = term if sign > 0 else -term
        else:
            total = total + term if sign > 0 else total - term
    return total


def first_moments(f):
    out = []
    for axis in range(3):
        out.append(signed_sum(sorted(((VEL[q][axis], f[q]) for q in range(Q) if VEL[q][axis]), key=lambda t: -t[0])))
    return out


def dot_c(q, vector):
    return signed_sum(sorted(((VEL[q][a], vector[a]) for a in range(3) if VEL[q][a]), key=lambda t: -t[0]))


def macroscopic(f):
    rho = functools.reduce(lambda a, b: a + b, f)
    mom = first_moments(f)
    inv = 1.0 / rho
    u = [m * inv for m in mom]
    speed = u[0] * u[0] + u[1] * u[1] + u[2] * u[2]
    return rho, u, speed


def collide(f, s, lab):
    rho, u, speed = macroscopic(f)
    rate = jnp.where(lab == 4.0, 1.0, OMEGA)
    inlet = lab == 3.0
    free = 1.0 - s
    keep = free * (1.0 - rate)
    gain = free * rate * rho
    base = 1.0 - 1.5 * speed
    post = [None] * Q
    for q in range(Q):
        o = OPP[q]
        if o < q:
            continue
        scaled = gain * WEIGHT[q]
        if q == 0:
            post[0] = (keep + s) * f[0] + scaled * base
            continue
        along = dot_c(q, u)
        even = scaled * (base + 4.5 * along * along)
        odd = scaled * (3.0 * along)
        post[q] = keep * f[q] + s * f[o] + (even + odd)
        post[o] = keep * f[o] + s * f[q] + (even - odd)
    return [jnp.where(inlet, inlet_value(q), post[q]) for q in range(Q)], rho, u, speed


def pull_back(lam, f, s, lab):
    rho, u, speed = macroscopic(f)
    rate = jnp.where(lab == 4.0, 1.0, OMEGA)
    inlet = lab == 3.0
    lam = [jnp.where(inlet, 0.0, v) for v in lam]
    wsum = [None] * Q
    s0 = WEIGHT[0] * lam[0]
    axis_sum = functools.reduce(lambda a, b: a + b, [lam[q] for q in range(1, 7)])
    diag_sum = functools.reduce(lambda a, b: a + b, [lam[q] for q in range(7, Q)])
    s0 = s0 + WEIGHT[1] * axis_sum + WEIGHT[7] * diag_sum
    s1, tens = [], {}
    for a in range(3):
        near = signed_sum(sorted(((VEL[q][a], lam[q]) for q in range(1, 7) if VEL[q][a]), key=lambda t: -t[0]))
        far = signed_sum(sorted(((VEL[q][a], lam[q]) for q in range(7, Q) if VEL[q][a]), key=lambda t: -t[0]))
        s1.append(WEIGHT[1] * near + WEIGHT[7] * far)
        near = functools.reduce(lambda x, y: x + y, [lam[q] for q in range(1, 7) if VEL[q][a]])
        far = functools.reduce(lambda x, y: x + y, [lam[q] for q in range(7, Q) if VEL[q][a]])
        tens[a, a] = WEIGHT[1] * near + WEIGHT[7] * far
    for a in range(3):
        for b in range(a + 1, 3):
            cross = signed_sum(sorted(((VEL[q][a] * VEL[q][b], lam[q]) for q in range(7, Q) if VEL[q][a] * VEL[q][b]), key=lambda t: -t[0]))
            tens[a, b] = tens[b, a] = WEIGHT[7] * cross
    tu = [tens[a, 0] * u[0] + tens[a, 1] * u[1] + tens[a, 2] * u[2] for a in range(3)]
    utu = tu[0] * u[0] + tu[1] * u[1] + tu[2] * u[2]
    free = 1.0 - s
    by_rho = s0 * (1.0 + 1.5 * speed) - 4.5 * utu
    by_mom = [3.0 * s1[a] + 9.0 * tu[a] - 3.0 * u[a] * s0 for a in range(3)]
    keep = free * (1.0 - rate)
    gain = free * rate
    g0 = gain * by_rho
    gm = [gain * by_mom[a] for a in range(3)]
    out = [None] * Q
    bounce = lam[0] * f[0]
    plain = lam[0] * f[0]
    for q in range(Q):
        o = OPP[q]
        if o < q:
            continue
        if q == 0:
            out[0] = (keep + s) * lam[0] + g0
            continue
        along = dot_c(q, gm)
        out[q] = keep * lam[q] + s * lam[o] + (g0 + along)
        out[o] = keep * lam[o] + s * lam[q] + (g0 - along)
        bounce = bounce + (lam[q] * f[o] + lam[o] * f[q])
        plain = plain + (lam[q] * f[q] + lam[o] * f[o])
    s1u = s1[0] * u[0] + s1[1] * u[1] + s1[2] * u[2]
    at_eq = rho * (s0 * (1.0 - 1.5 * speed) + 3.0 * s1u + 4.5 * utu)
    by_s = bounce - (1.0 - rate) * plain - rate * at_eq
    return out, by_s, rho, u, speed


def shifted(value, dx, dy):
    if dx:
        value = pltpu.roll(value, dx % value.shape[1], 1)
    if dy:
        value = pltpu.roll(value, dy % value.shape[0], 0)
    return value


def tiles(rows):
    return [pl.ds(8 * t, 8) for t in range(rows // 8)]


def pick(odd, first, second):
    return jnp.where(odd, second, first)


def write_pair(odd, to_pair, to_other, rising, falling):
    to_pair[...] = pick(odd, rising, falling)
    to_other[...] = pick(odd, falling, rising)


def kernel_pack(odd_y, pop, cell, edge_pair, edge_other):
    own = pop.shape[1]
    oy = odd_y[0] == 1
    for i in range(Q + 2):
        ref = pop.at[i] if i < Q else cell.at[i - Q]
        write_pair(oy, edge_pair.at[i], edge_other.at[i], ref[own - HALO : own, :], ref[0:HALO, :])


def send_first(odd, f, s, label, mid, pair, other, t, r):
    out, _, _, _ = collide(f, s, label)
    moved = [shifted(out[q], VEL[q][0], 0) for q in range(Q)]
    for i, q in enumerate(FLAT):
        mid[i, t, :] = moved[q]
    mid[len(FLAT), t, :] = s
    mid[len(FLAT) + 1, t, :] = label
    for i in range(len(RISE)):
        write_pair(odd, pair.at[i, r, :], other.at[i, r, :], moved[RISE[i]], moved[FALL[i]])


def kernel_one(odd_z, pop, cell, mid, pair, other):
    for t in tiles(pop.shape[1]):
        send_first(odd_z[0] == 1, [pop[q, t, :] for q in range(Q)], cell[0, t, :], cell[1, t, :], mid, pair, other, t, t)


def kernel_edge(odd_z, odd_y, edge_pair, edge_other, pair_in, other_in, mid, pair, other, tile):
    rows = pair.shape[1]
    oy = odd_y[0] == 1
    for i in range(Q + 2):
        a, b = edge_pair[i], edge_other[i]
        tile[i, :HALO, :] = pick(oy, a, b)
        tile[i, HALO:, :] = pick(oy, b, a)
    r = pl.ds(rows - 2 * HALO, 2 * HALO)
    f = [tile[q] for q in range(Q)]
    send_first(odd_z[0] == 1, f, tile[Q], tile[Q + 1], mid, pair, other, slice(None), r)


def kernel_two(odd_p, mid, pair, other, mid_e, field, mom, to_pair, to_other, part, raw, post):
    rows = field.shape[1]
    own = rows - 2 * HALO
    odd = odd_p[0] == 1
    for q in range(Q):
        cz = VEL[q][2]
        if cz == 0:
            raw[:own, :] = mid[FLAT.index(q)]
            raw[own:, :] = mid_e[FLAT.index(q)]
            value = raw[...]
        elif cz == 1:
            i = RISE.index(q)
            value = pick(odd, other[i], pair[i])
        else:
            i = FALL.index(q)
            value = pick(odd, pair[i], other[i])
        field[q] = shifted(value, 0, VEL[q][1])
    for i in (0, 1):
        field[Q + i, :own, :] = mid[len(FLAT) + i]
        field[Q + i, own:, :] = mid_e[len(FLAT) + i]
    total = None
    for t in tiles(rows):
        s = field[Q, t, :]
        out, rho, u, speed = collide([field[q, t, :] for q in range(Q)], s, field[Q + 1, t, :])
        for q in range(Q):
            post[q, t, :] = out[q]
        if t.start < own:
            e = (1.0 - s) * (rho * speed)
            total = e if total is None else total + e
    part[...] = total
    results = []
    for group in (FLAT, RISE, FALL):
        sums = [None, None, None]
        for q in group:
            cx, cy, _ = VEL[q]
            v = shifted(post[q], cx, cy)
            for k, sign in ((0, 1), (1, cx), (2, cy)):
                if sign:
                    if sums[k] is None:
                        sums[k] = v if sign > 0 else -v
                    else:
                        sums[k] = sums[k] + v if sign > 0 else sums[k] - v
        results.append(sums)
    for k in range(3):
        mom[k] = results[0][k]
        write_pair(odd, to_pair.at[k], to_other.at[k], results[1][k], results[2][k])


def kernel_three(odd_p, mom, pair, other, field, part, mine, to_pair, to_other, kinetic, out):
    rows = mom.shape[1]
    own = rows - 2 * HALO
    odd = odd_p[0] == 1
    total = part[...]
    for t in tiles(rows):
        below = [pick(odd, other[k, t, :], pair[k, t, :]) for k in range(3)]
        above = [pick(odd, pair[k, t, :], other[k, t, :]) for k in range(3)]
        rho = mom[0, t, :] + below[0] + above[0]
        inv = 1.0 / rho
        ux = (mom[1, t, :] + below[1] + above[1]) * inv
        uy = (mom[2, t, :] + below[2] + above[2]) * inv
        uz = (below[0] - above[0]) * inv
        speed = ux * ux + uy * uy + uz * uz
        free = 1.0 - field[Q, t, :]
        two = 2.0 * free
        ax, ay, az, b = two * ux, two * uy, two * uz, free * speed
        mine[0, t, :] = ax
        mine[1, t, :] = ay
        mine[2, t, :] = b
        to_pair[0, t, :] = ax
        to_pair[1, t, :] = ay
        to_other[0, t, :] = ax
        to_other[1, t, :] = ay
        write_pair(odd, to_pair.at[2, t, :], to_other.at[2, t, :], -az - b, az - b)
        if t.start < own:
            k = rho * speed
            kinetic[t, :] = k
            total = total + free * k
    half = total.shape[1] // 2
    out[...] = total[:, :half] + total[:, half:]


def kernel_four(odd_p, field, mine, pair, other, kinetic, energy, flat, to_pair, to_other, lam, adj):
    rows = field.shape[1]
    own = rows - 2 * HALO
    odd = odd_p[0] == 1
    low = [pick(odd, other[k], pair[k]) for k in range(3)]
    high = [pick(odd, pair[k], other[k]) for k in range(3)]
    for q in range(Q):
        cx, cy, cz = VEL[q]
        ref = {0: mine, 1: high, -1: low}[cz]
        value = ref[2]
        if cz == 0:
            value = -value
        if cx:
            value = value + ref[0] if cx > 0 else value - ref[0]
        if cy:
            value = value + ref[1] if cy > 0 else value - ref[1]
        lam[q] = shifted(value, -cx, -cy)
    for t in tiles(rows):
        s = field[Q, t, :]
        out, by_s, rho, u, speed = pull_back(
            [lam[q, t, :] for q in range(Q)], [field[q, t, :] for q in range(Q)], s, field[Q + 1, t, :]
        )
        free = 1.0 - s
        two = [2.0 * free * u[a] for a in range(3)]
        less = free * speed
        for q in range(Q):
            e = out[q] - less
            adj[q, t, :] = e + dot_c(q, two) if q else e
        if t.start < own:
            flat[len(FLAT), t, :] = by_s - rho * speed - kinetic[t, :]

    def pulled(q):
        return shifted(adj[q], -VEL[q][0], -VEL[q][1])[:own]

    for i, q in enumerate(FLAT):
        flat[i] = pulled(q)
    for i in range(len(RISE)):
        write_pair(odd, to_pair.at[i], to_other.at[i], pulled(FALL[i]), pulled(RISE[i]))


def kernel_five(cells, odd_z, pop, cell, flat, pair, other, energy, sens_h, out_h, sens, out, sems):
    own = pop.shape[1]
    odd = odd_z[0] == 1
    copies = []
    scale = cells / jnp.sum(energy[...], keepdims=True)
    scale = jnp.broadcast_to(scale, (8, pop.shape[2]))
    for t in tiles(own):
        s, label = cell[0, t, :], cell[1, t, :]
        lam = []
        for q in range(Q):
            if VEL[q][2] == 0:
                lam.append(flat[FLAT.index(q), t, :])
            elif VEL[q][2] == 1:
                i = RISE.index(q)
                lam.append(pick(odd, pair[i, t, :], other[i, t, :]))
            else:
                i = FALL.index(q)
                lam.append(pick(odd, other[i, t, :], pair[i, t, :]))
        grads, by_s, _, _, _ = pull_back(lam, [pop[q, t, :] for q in range(Q)], s, label)
        for q in range(Q):
            out[q, t, :] = grads[q] * scale
        sens[t, :] = jnp.where(label == 1.0, (by_s + flat[len(FLAT), t, :]) * scale, 0.0)
        n = t.start // 8
        copies.append(pltpu.make_async_copy(out.at[:, t, :], out_h.at[:, t, :], sems.at[n]))
        copies[-1].start()
    copies.append(pltpu.make_async_copy(sens, sens_h, sems.at[own // 8]))
    copies[-1].start()
    for c in copies:
        c.wait()


def call(kernel, shapes, scratch, flags, *args, hbm_out=False, sems=0, aliases=None):
    fast = pl.BlockSpec(memory_space=pltpu.VMEM)
    slow = pl.BlockSpec(memory_space=pltpu.HBM)
    return pl.pallas_call(
        kernel,
        out_shape=[jax.ShapeDtypeStruct(s, jnp.float32) for s in shapes],
        in_specs=[pl.BlockSpec(memory_space=pltpu.SMEM)] * len(flags)
        + [fast] * len(args),
        out_specs=[slow if hbm_out else fast] * len(shapes),
        scratch_shapes=[pltpu.VMEM(s, jnp.float32) for s in scratch]
        + ([pltpu.SemaphoreType.DMA((sems,))] if sems else []),
        input_output_aliases=aliases or {},
        compiler_params=pltpu.CompilerParams(vmem_limit_bytes=16 * 1024 * 1024),
    )(*flags, *args)


def summed(value, axes, groups):
    count = lax.axis_size(axes)
    if groups is None:
        return value
    for bits in groups:
        masks = [0]
        for bit in bits:
            masks += [m | bit for m in masks]
        parts = [lax.ppermute(value, axes, [(i, i ^ m) for i in range(count)]) for m in masks[1:]]
        value = functools.reduce(lambda a, b: a + b, parts, value)
    return value


def doublings(count):
    return [1 << b for b in range(count.bit_length() - 1)]


def sum_order(planes, chunks):
    y_bits = doublings(chunks)
    z_bits = [chunks * d for d in doublings(planes)]
    if 2 ** len(y_bits) != chunks or 2 ** len(z_bits) != planes:
        return None, None
    first = z_bits[-1:]
    rest = z_bits[:-1]
    late = [y_bits[1:] + rest[1:2]] + [[b] for b in rest[2:]] + [rest[:1], y_bits[:1]]
    return [g for g in [first] if g], [g for g in late if g]


class Layout:
    def __init__(self, planes, chunks):
        self.planes, self.chunks = planes, chunks
        self.bricks = [(p, k) for p in range(planes) for k in range(chunks)]
        self.swapped = planes % 2 == 0 and chunks % 2 == 0

    def start(self, p, k):
        return (p % self.planes) * self.chunks + k % self.chunks

    def home(self, p, k):
        p, k = p % self.planes, k % self.chunks
        if not self.swapped:
            return self.start(p, k)
        return self.start(p - p % 2 + (k + ALPHA) % 2, k - k % 2 + (p + BETA) % 2)

    def moves(self, source, target):
        side = lambda p: 1 - 2 * (p % 2)
        still = [(source(p, k), target(p, k)) for p, k in self.bricks]
        pair = [(source(p, k), target(p + side(p), k)) for p, k in self.bricks]
        other = [(source(p, k), target(p - side(p), k)) for p, k in self.bricks]
        return still, pair, other


def on_device(populations, solid_fraction, labels):
    _, _, own, wide = populations.shape
    rows = own + 2 * HALO
    axes = ("gz", "gy")
    planes, chunks = lax.axis_size("gz"), lax.axis_size("gy")
    layout = Layout(planes, chunks)
    flag = lambda axis: (lax.axis_index(axis) % 2).astype(jnp.int32).reshape(1)
    odd_z, odd_y = flag("gz"), flag("gy")
    odd_p = (odd_y + BETA) % 2 if layout.swapped else odd_z
    pop = populations.reshape(Q, own, wide)
    frac = solid_fraction.reshape(own, wide)
    lab = labels.reshape(own, wide)
    whole = lambda n: (n, rows, wide)
    less = lambda n: (n, own, wide)
    edge = lambda n: (n, 2 * HALO, wide)

    mixed = jnp.where(lab == 1, frac, jnp.where(lab == 2, jnp.float32(1.0), jnp.float32(0.0)))
    cell = jnp.stack([mixed, lab.astype(jnp.float32)])
    edge_a, edge_b = call(kernel_pack, [(Q + 2, HALO, wide)] * 2, [], [odd_y], pop, cell)
    side = lambda k: 1 - 2 * (k % 2)
    edge_a = lax.ppermute(edge_a, "gy", [(k, (k + side(k)) % chunks) for k in range(chunks)])
    edge_b = lax.ppermute(edge_b, "gy", [(k, (k - side(k)) % chunks) for k in range(chunks)])
    mid, pair, other = call(kernel_one, [less(11), whole(5), whole(5)], [], [odd_z], pop, cell)
    still_p, pair_p, other_p = layout.moves(layout.start, layout.home)
    mid = lax.ppermute(mid, axes, still_p)
    mid_e, pair, other = call(
        kernel_edge,
        [edge(11), whole(5), whole(5)],
        [edge(Q + 2)],
        [odd_z, odd_y],
        edge_a,
        edge_b,
        pair,
        other,
        aliases={4: 1, 5: 2},
    )
    mid_e = lax.ppermute(mid_e, axes, still_p)
    other = lax.ppermute(other, axes, other_p)
    pair = lax.ppermute(pair, axes, pair_p)
    field, mom, pair, other, part = call(
        kernel_two,
        [whole(Q + 2), whole(3), whole(3), whole(3), (8, wide)],
        [(rows, wide), whole(Q)],
        [odd_p],
        mid,
        pair,
        other,
        mid_e,
    )
    _, pair_p, other_p = layout.moves(layout.home, layout.home)
    other = lax.ppermute(other, axes, other_p)
    pair = lax.ppermute(pair, axes, pair_p)
    mine, pair, other, kinetic, energy = call(
        kernel_three,
        [whole(3), whole(3), whole(3), (own, wide), (8, wide // 2)],
        [],
        [odd_p],
        mom,
        pair,
        other,
        field,
        part,
    )
    other = lax.ppermute(other, axes, other_p)
    pair = lax.ppermute(pair, axes, pair_p)
    early, late = sum_order(planes, chunks)
    if early is None:
        energy = lax.psum(energy, axes)
    energy = summed(energy, axes, early)
    flat, pair, other = call(
        kernel_four,
        [less(10), less(5), less(5)],
        [whole(Q), whole(Q)],
        [odd_p],
        field,
        mine,
        pair,
        other,
        kinetic,
        energy,
    )
    still_p, pair_p, other_p = layout.moves(layout.home, layout.start)
    energy = summed(energy, axes, late)
    pair = lax.ppermute(pair, axes, pair_p)
    other = lax.ppermute(other, axes, other_p)
    flat = lax.ppermute(flat, axes, still_p)
    cells = float(STEPS * own * wide * populations.shape[1] * planes * chunks)
    sens, out = call(
        functools.partial(kernel_five, cells),
        [(own, wide), less(Q)],
        [(own, wide), less(Q)],
        [odd_z],
        pop,
        cell,
        flat,
        pair,
        other,
        energy,
        hbm_out=True,
        sems=own // 8 + 1,
    )
    return sens.reshape(solid_fraction.shape), out.reshape(populations.shape)


def solution(mesh):
    in_specs = (P(None, "gz", "gy", None), P("gz", "gy", None), P("gz", "gy", None))
    out_specs = (P("gz", "gy", None), P(None, "gz", "gy", None))
    return jax.shard_map(on_device, mesh=mesh, in_specs=in_specs, out_specs=out_specs, check_vma=False)
```

```python
import functools

import jax
import jax.numpy as jnp
from jax import lax
from jax.experimental import pallas as pl
from jax.experimental.pallas import tpu as pltpu
from jax.sharding import PartitionSpec as P

STEPS = 2
OMEGA = 0.9
INLET_SPEED = 0.05
HALO = 4
ALPHA, BETA = 0, 1


def velocity_table():
    velocities = [(0, 0, 0)]
    for axis in range(3):
        for sign in (1, -1):
            vector = [0, 0, 0]
            vector[axis] = sign
            velocities.append(tuple(vector))
    for first in range(3):
        for second in range(first + 1, 3):
            for sign_a in (1, -1):
                for sign_b in (1, -1):
                    vector = [0, 0, 0]
                    vector[first] = sign_a
                    vector[second] = sign_b
                    velocities.append(tuple(vector))
    weights = [1.0 / 3.0] + [1.0 / 18.0] * 6 + [1.0 / 36.0] * 12
    opposite = [velocities.index(tuple((-e for e in vector))) for vector in velocities]
    return (velocities, weights, opposite)


VEL, WEIGHT, OPP = velocity_table()
Q = len(VEL)
FLAT = [q for q in range(Q) if VEL[q][2] == 0]
RISE = [q for q in range(Q) if VEL[q][2] == 1]
FALL = [q for q in range(Q) if VEL[q][2] == -1]


def inlet_value(q):
    along = VEL[q][2] * INLET_SPEED
    return WEIGHT[q] * (1.0 + 3.0 * along + 4.5 * along * along - 1.5 * INLET_SPEED * INLET_SPEED)


def signed_sum(terms):
    total = None
    for sign, term in terms:
        if total is None:
            total = term if sign > 0 else -term
        else:
            total = total + term if sign > 0 else total - term
    return total


def first_moments(f):
    out = []
    for axis in range(3):
        out.append(signed_sum(sorted(((VEL[q][axis], f[q]) for q in range(Q) if VEL[q][axis]), key=lambda t: -t[0])))
    return out


def dot_c(q, vector):
    return signed_sum(sorted(((VEL[q][a], vector[a]) for a in range(3) if VEL[q][a]), key=lambda t: -t[0]))


def macroscopic(f):
    rho = functools.reduce(lambda a, b: a + b, f)
    mom = first_moments(f)
    inv = 1.0 / rho
    u = [m * inv for m in mom]
    speed = u[0] * u[0] + u[1] * u[1] + u[2] * u[2]
    return rho, u, speed


def collide(f, s, lab):
    rho, u, speed = macroscopic(f)
    rate = jnp.where(lab == 4.0, 1.0, OMEGA)
    inlet = lab == 3.0
    free = 1.0 - s
    keep = free * (1.0 - rate)
    gain = free * rate * rho
    base = 1.0 - 1.5 * speed
    post = [None] * Q
    for q in range(Q):
        o = OPP[q]
        if o < q:
            continue
        scaled = gain * WEIGHT[q]
        if q == 0:
            post[0] = (keep + s) * f[0] + scaled * base
            continue
        along = dot_c(q, u)
        even = scaled * (base + 4.5 * along * along)
        odd = scaled * (3.0 * along)
        post[q] = keep * f[q] + s * f[o] + (even + odd)
        post[o] = keep * f[o] + s * f[q] + (even - odd)
    return [jnp.where(inlet, inlet_value(q), post[q]) for q in range(Q)], rho, u, speed


def total(terms):
    return functools.reduce(lambda a, b: a + b, terms)


def by_moments(lam, group, u, speed):
    near = [q for q in group if 0 < q < 7]
    far = [q for q in group if q >= 7]

    def weighted(sign):
        out = None
        for weight, part in ((WEIGHT[1], near), (WEIGHT[7], far)):
            terms = sorted(((sign(VEL[q]), lam[q]) for q in part if sign(VEL[q])), key=lambda t: -t[0])
            if terms:
                term = weight * signed_sum(terms)
                out = term if out is None else out + term
        return out

    s0 = weighted(lambda c: 1)
    if 0 in group:
        s0 = s0 + WEIGHT[0] * lam[0]
    s1 = [weighted(lambda c: c[a]) for a in range(3)]
    tens = {(a, b): weighted(lambda c: c[a] * c[b]) for a in range(3) for b in range(3)}
    plus = lambda terms: total(terms) if terms else None
    tu = [plus([tens[a, b] * u[b] for b in range(3) if tens[a, b] is not None]) for a in range(3)]
    utu = total([tu[a] * u[a] for a in range(3) if tu[a] is not None])
    by_rho = s0 * (1.0 + 1.5 * speed) - 4.5 * utu
    by_mom = []
    for a in range(3):
        value = -3.0 * u[a] * s0
        if tu[a] is not None:
            value = value + 9.0 * tu[a]
        if s1[a] is not None:
            value = value + 3.0 * s1[a]
        by_mom.append(value)
    s1u = total([s1[a] * u[a] for a in range(3) if s1[a] is not None])
    along = s0 * (1.0 - 1.5 * speed) + 3.0 * s1u + 4.5 * utu
    return by_rho, by_mom, along


def rates(s, lab):
    rate = jnp.where(lab == 4.0, 1.0, OMEGA)
    free = 1.0 - s
    return rate, free * (1.0 - rate), free * rate


def spread(lam, group, s, keep, g0, gm):
    out = {}
    for q in group:
        o = OPP[q]
        if q == 0:
            out[0] = (keep + s) * lam[0] + g0
        elif q < o:
            along = dot_c(q, gm)
            out[q] = keep * lam[q] + s * lam[o] + (g0 + along)
            out[o] = keep * lam[o] + s * lam[q] + (g0 - along)
    return out


def pull_back(lam, f, s, lab, group):
    rho, u, speed = macroscopic(f)
    rate, keep, gain = rates(s, lab)
    inlet = lab == 3.0
    lam = [jnp.where(inlet, 0.0, v) for v in lam]
    by_rho, by_mom, along = by_moments(lam, range(Q), u, speed)
    g0 = gain * by_rho
    gm = [gain * by_mom[a] for a in range(3)]
    out = spread(lam, group, s, keep, g0, gm)
    bounce = lam[0] * f[0]
    plain = lam[0] * f[0]
    for q in range(1, Q):
        o = OPP[q]
        if q < o:
            bounce = bounce + (lam[q] * f[o] + lam[o] * f[q])
            plain = plain + (lam[q] * f[q] + lam[o] * f[o])
    by_s = bounce - (1.0 - rate) * plain - rate * (rho * along)
    return out, by_s, rho, u, speed, (g0, gm[0], gm[1])


def shifted(value, dx, dy):
    if dx:
        value = pltpu.roll(value, dx % value.shape[1], 1)
    if dy:
        value = pltpu.roll(value, dy % value.shape[0], 0)
    return value


def tiles(rows):
    return [pl.ds(8 * t, 8) for t in range(rows // 8)]


def pick(odd, first, second):
    return jnp.where(odd, second, first)


def write_pair(odd, to_pair, to_other, rising, falling):
    to_pair[...] = pick(odd, rising, falling)
    to_other[...] = pick(odd, falling, rising)


def kernel_pack(odd_y, pop, cell, edge_pair, edge_other):
    own = pop.shape[1]
    oy = odd_y[0] == 1
    for i in range(Q + 2):
        ref = pop.at[i] if i < Q else cell.at[i - Q]
        write_pair(oy, edge_pair.at[i], edge_other.at[i], ref[own - HALO : own, :], ref[0:HALO, :])


def send_first(odd, f, s, label, mid, pair, other, t, r):
    out, _, _, _ = collide(f, s, label)
    moved = [shifted(out[q], VEL[q][0], 0) for q in range(Q)]
    for i, q in enumerate(FLAT):
        mid[i, t, :] = moved[q]
    mid[len(FLAT), t, :] = s
    mid[len(FLAT) + 1, t, :] = label
    for i in range(len(RISE)):
        write_pair(odd, pair.at[i, r, :], other.at[i, r, :], moved[RISE[i]], moved[FALL[i]])


def kernel_one(odd_z, pop, cell, mid, pair, other):
    for t in tiles(pop.shape[1]):
        send_first(odd_z[0] == 1, [pop[q, t, :] for q in range(Q)], cell[0, t, :], cell[1, t, :], mid, pair, other, t, t)


def kernel_edge(odd_z, odd_y, edge_pair, edge_other, pair_in, other_in, mid, pair, other, tile):
    rows = pair.shape[1]
    oy = odd_y[0] == 1
    for i in range(Q + 2):
        a, b = edge_pair[i], edge_other[i]
        tile[i, :HALO, :] = pick(oy, a, b)
        tile[i, HALO:, :] = pick(oy, b, a)
    r = pl.ds(rows - 2 * HALO, 2 * HALO)
    f = [tile[q] for q in range(Q)]
    send_first(odd_z[0] == 1, f, tile[Q], tile[Q + 1], mid, pair, other, slice(None), r)


def kernel_two(odd_p, mid, pair, other, mid_e, field, mom, to_pair, to_other, part, raw, post):
    rows = field.shape[1]
    own = rows - 2 * HALO
    odd = odd_p[0] == 1
    for q in range(Q):
        cz = VEL[q][2]
        if cz == 0:
            raw[:own, :] = mid[FLAT.index(q)]
            raw[own:, :] = mid_e[FLAT.index(q)]
            value = raw[...]
        elif cz == 1:
            i = RISE.index(q)
            value = pick(odd, other[i], pair[i])
        else:
            i = FALL.index(q)
            value = pick(odd, pair[i], other[i])
        field[q] = shifted(value, 0, VEL[q][1])
    for i in (0, 1):
        field[Q + i, :own, :] = mid[len(FLAT) + i]
        field[Q + i, own:, :] = mid_e[len(FLAT) + i]
    total = None
    for t in tiles(rows):
        s = field[Q, t, :]
        out, rho, u, speed = collide([field[q, t, :] for q in range(Q)], s, field[Q + 1, t, :])
        for q in range(Q):
            post[q, t, :] = out[q]
        if t.start < own:
            e = (1.0 - s) * (rho * speed)
            total = e if total is None else total + e
    part[...] = total
    results = []
    for group in (FLAT, RISE, FALL):
        sums = [None, None, None]
        for q in group:
            cx, cy, _ = VEL[q]
            v = shifted(post[q], cx, cy)
            for k, sign in ((0, 1), (1, cx), (2, cy)):
                if sign:
                    if sums[k] is None:
                        sums[k] = v if sign > 0 else -v
                    else:
                        sums[k] = sums[k] + v if sign > 0 else sums[k] - v
        results.append(sums)
    for k in range(3):
        mom[k] = results[0][k]
        write_pair(odd, to_pair.at[k], to_other.at[k], results[1][k], results[2][k])


def kernel_three(odd_p, mom, pair, other, field, part, mine, to_pair, to_other, kinetic, out):
    rows = mom.shape[1]
    own = rows - 2 * HALO
    odd = odd_p[0] == 1
    total = part[...]
    for t in tiles(rows):
        below = [pick(odd, other[k, t, :], pair[k, t, :]) for k in range(3)]
        above = [pick(odd, pair[k, t, :], other[k, t, :]) for k in range(3)]
        rho = mom[0, t, :] + below[0] + above[0]
        inv = 1.0 / rho
        ux = (mom[1, t, :] + below[1] + above[1]) * inv
        uy = (mom[2, t, :] + below[2] + above[2]) * inv
        uz = (below[0] - above[0]) * inv
        speed = ux * ux + uy * uy + uz * uz
        free = 1.0 - field[Q, t, :]
        two = 2.0 * free
        ax, ay, az, b = two * ux, two * uy, two * uz, free * speed
        mine[0, t, :] = ax
        mine[1, t, :] = ay
        mine[2, t, :] = b
        to_pair[0, t, :] = ax
        to_pair[1, t, :] = ay
        to_other[0, t, :] = ax
        to_other[1, t, :] = ay
        write_pair(odd, to_pair.at[2, t, :], to_other.at[2, t, :], -az - b, az - b)
        if t.start < own:
            k = rho * speed
            kinetic[t, :] = k
            total = total + free * k
    half = total.shape[1] // 2
    out[...] = total[:, :half] + total[:, half:]


def fill_adjoint(lam, group, sources):
    for q in group:
        cx, cy, cz = VEL[q]
        ref = sources[cz]
        value = ref[2]
        if cz == 0:
            value = -value
        if cx:
            value = value + ref[0] if cx > 0 else value - ref[0]
        if cy:
            value = value + ref[1] if cy > 0 else value - ref[1]
        lam[q] = shifted(value, -cx, -cy)


def energy_part(q, out, two, less):
    e = out - less
    return e + dot_c(q, two) if q else e


def kernel_near(field, mine, flat, near, lam, adj):
    rows = field.shape[1]
    own = rows - 2 * HALO
    fill_adjoint(lam, FLAT, {0: mine})
    for t in tiles(rows):
        s, label = field[Q, t, :], field[Q + 1, t, :]
        rho, u, speed = macroscopic([field[q, t, :] for q in range(Q)])
        rate, keep, gain = rates(s, label)
        inlet = label == 3.0
        here = {q: jnp.where(inlet, 0.0, lam[q, t, :]) for q in FLAT}
        by_rho, by_mom, _ = by_moments(here, FLAT, u, speed)
        g0 = gain * by_rho
        gm = [gain * by_mom[a] for a in range(2)]
        near[0, t, :] = g0
        near[1, t, :] = gm[0]
        near[2, t, :] = gm[1]
        out = spread(here, FLAT, s, keep, g0, gm + [None])
        free = 1.0 - s
        two = [2.0 * free * u[a] for a in range(3)]
        less = free * speed
        for i, q in enumerate(FLAT):
            adj[i, t, :] = energy_part(q, out[q], two, less)
    for i, q in enumerate(FLAT):
        flat[i] = shifted(adj[i], -VEL[q][0], -VEL[q][1])[:own]


def kernel_four(odd_p, field, mine, pair, other, kinetic, near, late, to_pair, to_other, lam, adj):
    rows = field.shape[1]
    own = rows - 2 * HALO
    odd = odd_p[0] == 1
    low = [pick(odd, other[k], pair[k]) for k in range(3)]
    high = [pick(odd, pair[k], other[k]) for k in range(3)]
    fill_adjoint(lam, range(Q), {0: mine, 1: high, -1: low})
    for t in tiles(rows):
        s = field[Q, t, :]
        out, by_s, rho, u, speed, through = pull_back(
            [lam[q, t, :] for q in range(Q)],
            [field[q, t, :] for q in range(Q)],
            s,
            field[Q + 1, t, :],
            sorted(RISE + FALL),
        )
        free = 1.0 - s
        two = [2.0 * free * u[a] for a in range(3)]
        less = free * speed
        for q in RISE + FALL:
            adj[q, t, :] = energy_part(q, out[q], two, less)
        for k in range(3):
            late[k, t, :] = through[k] - near[k, t, :]
        if t.start < own:
            late[3, t, :] = by_s - rho * speed - kinetic[t, :]
        else:
            late[3, t, :] = jnp.zeros_like(s)

    def pulled(q):
        return shifted(adj[q], -VEL[q][0], -VEL[q][1])[:own]

    for i in range(len(RISE)):
        write_pair(odd, to_pair.at[i], to_other.at[i], pulled(FALL[i]), pulled(RISE[i]))


def kernel_five(cells, odd_z, pop, cell, flat, late, pair, other, energy, sens_h, out_h, sens, out, level, sems):
    own = pop.shape[1]
    odd = odd_z[0] == 1
    copies = []
    for i, q in enumerate(FLAT):
        cx, cy, _ = VEL[q]
        value = late[0]
        if cx:
            value = value + late[1] if cx > 0 else value - late[1]
        if cy:
            value = value + late[2] if cy > 0 else value - late[2]
        level[i] = flat[i] + shifted(value, -cx, -cy)[:own]
    scale = cells / jnp.sum(jnp.sum(energy[...], axis=0), keepdims=True)
    scale = jnp.broadcast_to(scale, (8, pop.shape[2]))
    for t in tiles(own):
        s, label = cell[0, t, :], cell[1, t, :]
        lam = []
        for q in range(Q):
            if VEL[q][2] == 0:
                lam.append(level[FLAT.index(q), t, :])
            elif VEL[q][2] == 1:
                i = RISE.index(q)
                lam.append(pick(odd, pair[i, t, :], other[i, t, :]))
            else:
                i = FALL.index(q)
                lam.append(pick(odd, other[i, t, :], pair[i, t, :]))
        grads, by_s, _, _, _, _ = pull_back(lam, [pop[q, t, :] for q in range(Q)], s, label, range(Q))
        for q in range(Q):
            out[q, t, :] = grads[q] * scale
        sens[t, :] = jnp.where(label == 1.0, (by_s + late[3, t, :]) * scale, 0.0)
        n = t.start // 8
        copies.append(pltpu.make_async_copy(out.at[:, t, :], out_h.at[:, t, :], sems.at[n]))
        copies[-1].start()
    copies.append(pltpu.make_async_copy(sens, sens_h, sems.at[own // 8]))
    copies[-1].start()
    for c in copies:
        c.wait()


def call(kernel, shapes, scratch, flags, *args, hbm_out=False, sems=0, aliases=None):
    fast = pl.BlockSpec(memory_space=pltpu.VMEM)
    slow = pl.BlockSpec(memory_space=pltpu.HBM)
    return pl.pallas_call(
        kernel,
        out_shape=[jax.ShapeDtypeStruct(s, jnp.float32) for s in shapes],
        in_specs=[pl.BlockSpec(memory_space=pltpu.SMEM)] * len(flags)
        + [fast] * len(args),
        out_specs=[slow if hbm_out else fast] * len(shapes),
        scratch_shapes=[pltpu.VMEM(s, jnp.float32) for s in scratch]
        + ([pltpu.SemaphoreType.DMA((sems,))] if sems else []),
        input_output_aliases=aliases or {},
        compiler_params=pltpu.CompilerParams(vmem_limit_bytes=16 * 1024 * 1024),
    )(*flags, *args)


class Layout:
    def __init__(self, planes, chunks):
        self.planes, self.chunks = planes, chunks
        self.bricks = [(p, k) for p in range(planes) for k in range(chunks)]
        self.swapped = planes % 2 == 0 and chunks % 2 == 0

    def start(self, p, k):
        return (p % self.planes) * self.chunks + k % self.chunks

    def home(self, p, k):
        p, k = p % self.planes, k % self.chunks
        if not self.swapped:
            return self.start(p, k)
        return self.start(p - p % 2 + (k + ALPHA) % 2, k - k % 2 + (p + BETA) % 2)

    def moves(self, source, target):
        side = lambda p: 1 - 2 * (p % 2)
        still = [(source(p, k), target(p, k)) for p, k in self.bricks]
        pair = [(source(p, k), target(p + side(p), k)) for p, k in self.bricks]
        other = [(source(p, k), target(p - side(p), k)) for p, k in self.bricks]
        return still, pair, other


def on_device(populations, solid_fraction, labels):
    _, _, own, wide = populations.shape
    rows = own + 2 * HALO
    axes = ("gz", "gy")
    planes, chunks = lax.axis_size("gz"), lax.axis_size("gy")
    layout = Layout(planes, chunks)
    flag = lambda axis: (lax.axis_index(axis) % 2).astype(jnp.int32).reshape(1)
    odd_z, odd_y = flag("gz"), flag("gy")
    odd_p = (odd_y + BETA) % 2 if layout.swapped else odd_z
    pop = populations.reshape(Q, own, wide)
    frac = solid_fraction.reshape(own, wide)
    lab = labels.reshape(own, wide)
    whole = lambda n: (n, rows, wide)
    less = lambda n: (n, own, wide)
    edge = lambda n: (n, 2 * HALO, wide)

    mixed = jnp.where(lab == 1, frac, jnp.where(lab == 2, jnp.float32(1.0), jnp.float32(0.0)))
    cell = jnp.stack([mixed, lab.astype(jnp.float32)])
    edge_a, edge_b = call(kernel_pack, [(Q + 2, HALO, wide)] * 2, [], [odd_y], pop, cell)
    side = lambda k: 1 - 2 * (k % 2)
    edge_a = lax.ppermute(edge_a, "gy", [(k, (k + side(k)) % chunks) for k in range(chunks)])
    edge_b = lax.ppermute(edge_b, "gy", [(k, (k - side(k)) % chunks) for k in range(chunks)])
    mid, pair, other = call(kernel_one, [less(11), whole(5), whole(5)], [], [odd_z], pop, cell)
    still_p, pair_p, other_p = layout.moves(layout.start, layout.home)
    mid = lax.ppermute(mid, axes, still_p)
    mid_e, pair, other = call(
        kernel_edge,
        [edge(11), whole(5), whole(5)],
        [edge(Q + 2)],
        [odd_z, odd_y],
        edge_a,
        edge_b,
        pair,
        other,
        aliases={4: 1, 5: 2},
    )
    mid_e = lax.ppermute(mid_e, axes, still_p)
    other = lax.ppermute(other, axes, other_p)
    pair = lax.ppermute(pair, axes, pair_p)
    field, mom, pair, other, part = call(
        kernel_two,
        [whole(Q + 2), whole(3), whole(3), whole(3), (8, wide)],
        [(rows, wide), whole(Q)],
        [odd_p],
        mid,
        pair,
        other,
        mid_e,
    )
    _, pair_p, other_p = layout.moves(layout.home, layout.home)
    other = lax.ppermute(other, axes, other_p)
    pair = lax.ppermute(pair, axes, pair_p)
    mine, pair, other, kinetic, energy = call(
        kernel_three,
        [whole(3), whole(3), whole(3), (own, wide), (8, wide // 2)],
        [],
        [odd_p],
        mom,
        pair,
        other,
        field,
        part,
    )
    other = lax.ppermute(other, axes, other_p)
    pair = lax.ppermute(pair, axes, pair_p)
    energy = jnp.broadcast_to(energy, (planes * chunks,) + energy.shape)
    energy = lax.all_to_all(energy, axes, 0, 0, tiled=True)
    flat, near = call(kernel_near, [less(9), whole(3)], [whole(Q), whole(9)], [], field, mine)
    late, pair, other = call(
        kernel_four,
        [whole(4), less(5), less(5)],
        [whole(Q), whole(Q)],
        [odd_p],
        field,
        mine,
        pair,
        other,
        kinetic,
        near,
    )
    still_p, pair_p, other_p = layout.moves(layout.home, layout.start)
    flat = lax.ppermute(flat, axes, still_p)
    pair = lax.ppermute(pair, axes, pair_p)
    other = lax.ppermute(other, axes, other_p)
    late = lax.ppermute(late, axes, still_p)
    cells = float(STEPS * own * wide * populations.shape[1] * planes * chunks)
    sens, out = call(
        functools.partial(kernel_five, cells),
        [(own, wide), less(Q)],
        [(own, wide), less(Q), less(9)],
        [odd_z],
        pop,
        cell,
        flat,
        late,
        pair,
        other,
        energy,
        hbm_out=True,
        sems=own // 8 + 1,
    )
    return sens.reshape(solid_fraction.shape), out.reshape(populations.shape)


def solution(mesh):
    in_specs = (P(None, "gz", "gy", None), P("gz", "gy", None), P("gz", "gy", None))
    out_specs = (P("gz", "gy", None), P(None, "gz", "gy", None))
    return jax.shard_map(on_device, mesh=mesh, in_specs=in_specs, out_specs=out_specs, check_vma=False)
```

```python
import functools

import jax
import jax.numpy as jnp
from jax import lax
from jax.experimental import pallas as pl
from jax.experimental.pallas import tpu as pltpu
from jax.sharding import PartitionSpec as P

STEPS = 2
OMEGA = 0.9
INLET_SPEED = 0.05
HALO = 4
ALPHA, BETA = 0, 1


def velocity_table():
    velocities = [(0, 0, 0)]
    for axis in range(3):
        for sign in (1, -1):
            vector = [0, 0, 0]
            vector[axis] = sign
            velocities.append(tuple(vector))
    for first in range(3):
        for second in range(first + 1, 3):
            for sign_a in (1, -1):
                for sign_b in (1, -1):
                    vector = [0, 0, 0]
                    vector[first] = sign_a
                    vector[second] = sign_b
                    velocities.append(tuple(vector))
    weights = [1.0 / 3.0] + [1.0 / 18.0] * 6 + [1.0 / 36.0] * 12
    opposite = [velocities.index(tuple((-e for e in vector))) for vector in velocities]
    return (velocities, weights, opposite)


VEL, WEIGHT, OPP = velocity_table()
Q = len(VEL)
FLAT = [q for q in range(Q) if VEL[q][2] == 0]
RISE = [q for q in range(Q) if VEL[q][2] == 1]
FALL = [q for q in range(Q) if VEL[q][2] == -1]


def inlet_value(q):
    along = VEL[q][2] * INLET_SPEED
    return WEIGHT[q] * (1.0 + 3.0 * along + 4.5 * along * along - 1.5 * INLET_SPEED * INLET_SPEED)


def signed_sum(terms):
    total = None
    for sign, term in terms:
        if total is None:
            total = term if sign > 0 else -term
        else:
            total = total + term if sign > 0 else total - term
    return total


def first_moments(f):
    out = []
    for axis in range(3):
        out.append(signed_sum(sorted(((VEL[q][axis], f[q]) for q in range(Q) if VEL[q][axis]), key=lambda t: -t[0])))
    return out


def dot_c(q, vector):
    return signed_sum(sorted(((VEL[q][a], vector[a]) for a in range(3) if VEL[q][a]), key=lambda t: -t[0]))


def macroscopic(f):
    rho = functools.reduce(lambda a, b: a + b, f)
    mom = first_moments(f)
    inv = 1.0 / rho
    u = [m * inv for m in mom]
    speed = u[0] * u[0] + u[1] * u[1] + u[2] * u[2]
    return rho, u, speed


def collide(f, s, lab):
    rho, u, speed = macroscopic(f)
    rate = jnp.where(lab == 4.0, 1.0, OMEGA)
    inlet = lab == 3.0
    free = 1.0 - s
    keep = free * (1.0 - rate)
    gain = free * rate * rho
    base = 1.0 - 1.5 * speed
    post = [None] * Q
    for q in range(Q):
        o = OPP[q]
        if o < q:
            continue
        scaled = gain * WEIGHT[q]
        if q == 0:
            post[0] = (keep + s) * f[0] + scaled * base
            continue
        along = dot_c(q, u)
        even = scaled * (base + 4.5 * along * along)
        odd = scaled * (3.0 * along)
        post[q] = keep * f[q] + s * f[o] + (even + odd)
        post[o] = keep * f[o] + s * f[q] + (even - odd)
    return [jnp.where(inlet, inlet_value(q), post[q]) for q in range(Q)], rho, u, speed


def total(terms):
    return functools.reduce(lambda a, b: a + b, terms)


def by_moments(lam, group, u, speed):
    near = [q for q in group if 0 < q < 7]
    far = [q for q in group if q >= 7]

    def weighted(sign):
        out = None
        for weight, part in ((WEIGHT[1], near), (WEIGHT[7], far)):
            terms = sorted(((sign(VEL[q]), lam[q]) for q in part if sign(VEL[q])), key=lambda t: -t[0])
            if terms:
                term = weight * signed_sum(terms)
                out = term if out is None else out + term
        return out

    s0 = weighted(lambda c: 1)
    if 0 in group:
        s0 = s0 + WEIGHT[0] * lam[0]
    s1 = [weighted(lambda c: c[a]) for a in range(3)]
    tens = {(a, b): weighted(lambda c: c[a] * c[b]) for a in range(3) for b in range(3)}
    plus = lambda terms: total(terms) if terms else None
    tu = [plus([tens[a, b] * u[b] for b in range(3) if tens[a, b] is not None]) for a in range(3)]
    utu = total([tu[a] * u[a] for a in range(3) if tu[a] is not None])
    by_rho = s0 * (1.0 + 1.5 * speed) - 4.5 * utu
    by_mom = []
    for a in range(3):
        value = -3.0 * u[a] * s0
        if tu[a] is not None:
            value = value + 9.0 * tu[a]
        if s1[a] is not None:
            value = value + 3.0 * s1[a]
        by_mom.append(value)
    s1u = total([s1[a] * u[a] for a in range(3) if s1[a] is not None])
    along = s0 * (1.0 - 1.5 * speed) + 3.0 * s1u + 4.5 * utu
    return by_rho, by_mom, along


def stored(field, t):
    return field[Q + 2, t, :], [field[Q + 3 + a, t, :] for a in range(3)], field[Q + 6, t, :]


def rates(s, lab):
    rate = jnp.where(lab == 4.0, 1.0, OMEGA)
    free = 1.0 - s
    return rate, free * (1.0 - rate), free * rate


def spread(lam, group, s, keep, g0, gm):
    out = {}
    for q in group:
        o = OPP[q]
        if q == 0:
            out[0] = (keep + s) * lam[0] + g0
        elif q < o:
            along = dot_c(q, gm)
            out[q] = keep * lam[q] + s * lam[o] + (g0 + along)
            out[o] = keep * lam[o] + s * lam[q] + (g0 - along)
    return out


def pull_back(lam, f, s, lab, group, known=None):
    rho, u, speed = known or macroscopic(f)
    rate, keep, gain = rates(s, lab)
    inlet = lab == 3.0
    lam = [jnp.where(inlet, 0.0, v) for v in lam]
    by_rho, by_mom, along = by_moments(lam, range(Q), u, speed)
    g0 = gain * by_rho
    gm = [gain * by_mom[a] for a in range(3)]
    out = spread(lam, group, s, keep, g0, gm)
    bounce = lam[0] * f[0]
    plain = lam[0] * f[0]
    for q in range(1, Q):
        o = OPP[q]
        if q < o:
            bounce = bounce + (lam[q] * f[o] + lam[o] * f[q])
            plain = plain + (lam[q] * f[q] + lam[o] * f[o])
    by_s = bounce - (1.0 - rate) * plain - rate * (rho * along)
    return out, by_s, rho, u, speed, (g0, gm[0], gm[1])


def shifted(value, dx, dy):
    if dx:
        value = pltpu.roll(value, dx % value.shape[1], 1)
    if dy:
        value = pltpu.roll(value, dy % value.shape[0], 0)
    return value


def tiles(rows):
    return [pl.ds(8 * t, 8) for t in range(rows // 8)]


def pick(odd, first, second):
    return jnp.where(odd, second, first)


def write_pair(odd, to_pair, to_other, rising, falling):
    to_pair[...] = pick(odd, rising, falling)
    to_other[...] = pick(odd, falling, rising)


def edge_rows(q, high):
    if q >= Q:
        return HALO - 1
    cy = VEL[q][1] if high else -VEL[q][1]
    return {0: HALO - 1, 1: HALO - 2, -1: HALO}[cy]


def edge_slots(high):
    slots, at = {}, 0
    for q in range(Q + 2):
        n = edge_rows(q, high)
        slots[q] = (at, n)
        at += n
    return slots, at


def kernel_one(odd_z, odd_y, pop, cell, edge_pair, edge_other, mid, pair, other, post):
    own = pop.shape[1]
    odd, oy = odd_z[0] == 1, odd_y[0] == 1
    for t in tiles(own):
        s, label = cell[0, t, :], cell[1, t, :]
        out, _, _, _ = collide([pop[q, t, :] for q in range(Q)], s, label)
        for q in range(Q):
            post[q, t, :] = shifted(out[q], VEL[q][0], 0)
        mid[len(FLAT), t, :] = s
        mid[len(FLAT) + 1, t, :] = label
    low_slots, size = edge_slots(True)
    high_slots, _ = edge_slots(False)
    field = lambda q: post.at[q] if q < Q else cell.at[q - Q]

    def fill(to_high, to_low):
        for q in range(Q + 2):
            at, n = low_slots[q]
            to_low[at : at + n, :] = field(q)[:n, :]
            at, n = high_slots[q]
            to_high[at : at + n, :] = field(q)[own - n : own, :]

    @pl.when(oy)
    def _():
        fill(edge_other, edge_pair)

    @pl.when(jnp.logical_not(oy))
    def _():
        fill(edge_pair, edge_other)

    for i, q in enumerate(FLAT):
        mid[i] = post[q]
    for i in range(len(RISE)):
        for t in tiles(own):
            write_pair(odd, pair.at[i, t, :], other.at[i, t, :], post[RISE[i], t, :], post[FALL[i], t, :])


def kernel_edge(odd_z, odd_y, edge_pair, edge_other, pair_in, other_in, mid, pair, other):
    rows = pair.shape[1]
    odd, oy = odd_z[0] == 1, odd_y[0] == 1
    from_high, size = edge_slots(True)
    from_low, _ = edge_slots(False)
    zeros = lambda n: [jnp.zeros((n, pair.shape[2]), jnp.float32)] if n else []

    def tile(q, high, low):
        at, n = from_high[q]
        top = [high[at : at + n, :]] + zeros(HALO - n)
        at, n = from_low[q]
        return jnp.concatenate(top + zeros(HALO - n) + [low[at : at + n, :]], axis=0)

    def build(high, low):
        for i, q in enumerate(FLAT + [Q, Q + 1]):
            mid[i] = tile(q, high, low)
        r = pl.ds(rows - 2 * HALO, 2 * HALO)
        for i in range(len(RISE)):
            write_pair(odd, pair.at[i, r, :], other.at[i, r, :], tile(RISE[i], high, low), tile(FALL[i], high, low))

    @pl.when(oy)
    def _():
        build(edge_other, edge_pair)

    @pl.when(jnp.logical_not(oy))
    def _():
        build(edge_pair, edge_other)


def kernel_two(odd_p, mid, pair, other, mid_e, field, mom, to_pair, to_other, part, raw, post):
    rows = field.shape[1]
    own = rows - 2 * HALO
    odd = odd_p[0] == 1
    for q in range(Q):
        cz = VEL[q][2]
        if cz == 0:
            raw[:own, :] = mid[FLAT.index(q)]
            raw[own:, :] = mid_e[FLAT.index(q)]
            value = raw[...]
        elif cz == 1:
            i = RISE.index(q)
            value = pick(odd, other[i], pair[i])
        else:
            i = FALL.index(q)
            value = pick(odd, pair[i], other[i])
        field[q] = shifted(value, 0, VEL[q][1])
    for i in (0, 1):
        field[Q + i, :own, :] = mid[len(FLAT) + i]
        field[Q + i, own:, :] = mid_e[len(FLAT) + i]
    total = None
    for t in tiles(rows):
        s = field[Q, t, :]
        out, rho, u, speed = collide([field[q, t, :] for q in range(Q)], s, field[Q + 1, t, :])
        for q in range(Q):
            post[q, t, :] = out[q]
        for i, value in enumerate([rho] + u + [speed]):
            field[Q + 2 + i, t, :] = value
        if t.start < own:
            e = (1.0 - s) * (rho * speed)
            total = e if total is None else total + e
    part[...] = total
    results = []
    for group in (FLAT, RISE, FALL):
        sums = [None, None, None]
        for q in group:
            cx, cy, _ = VEL[q]
            v = shifted(post[q], cx, cy)
            for k, sign in ((0, 1), (1, cx), (2, cy)):
                if sign:
                    if sums[k] is None:
                        sums[k] = v if sign > 0 else -v
                    else:
                        sums[k] = sums[k] + v if sign > 0 else sums[k] - v
        results.append(sums)
    for k in range(3):
        mom[k] = results[0][k]
        write_pair(odd, to_pair.at[k], to_other.at[k], results[1][k], results[2][k])


def kernel_three(odd_p, mom, pair, other, field, part, mine, to_pair, to_other, kinetic, out):
    rows = mom.shape[1]
    own = rows - 2 * HALO
    odd = odd_p[0] == 1
    total = part[...]
    for t in tiles(rows):
        below = [pick(odd, other[k, t, :], pair[k, t, :]) for k in range(3)]
        above = [pick(odd, pair[k, t, :], other[k, t, :]) for k in range(3)]
        rho = mom[0, t, :] + below[0] + above[0]
        inv = 1.0 / rho
        ux = (mom[1, t, :] + below[1] + above[1]) * inv
        uy = (mom[2, t, :] + below[2] + above[2]) * inv
        uz = (below[0] - above[0]) * inv
        speed = ux * ux + uy * uy + uz * uz
        free = 1.0 - field[Q, t, :]
        two = 2.0 * free
        ax, ay, az, b = two * ux, two * uy, two * uz, free * speed
        mine[0, t, :] = ax
        mine[1, t, :] = ay
        mine[2, t, :] = b
        to_pair[0, t, :] = ax
        to_pair[1, t, :] = ay
        to_other[0, t, :] = ax
        to_other[1, t, :] = ay
        write_pair(odd, to_pair.at[2, t, :], to_other.at[2, t, :], -az - b, az - b)
        if t.start < own:
            k = rho * speed
            kinetic[t, :] = k
            total = total + free * k
    half = total.shape[1] // 2
    out[...] = total[:, :half] + total[:, half:]


def fill_adjoint(lam, group, sources):
    for q in group:
        cx, cy, cz = VEL[q]
        ref = sources[cz]
        value = ref[2]
        if cz == 0:
            value = -value
        if cx:
            value = value + ref[0] if cx > 0 else value - ref[0]
        if cy:
            value = value + ref[1] if cy > 0 else value - ref[1]
        lam[q] = shifted(value, -cx, -cy)


def energy_part(q, out, two, less):
    e = out - less
    return e + dot_c(q, two) if q else e


def kernel_near(field, mine, energy, flat, near, shares, lam, adj, block, sems):
    for i in range(block.shape[0]):
        block[i] = energy[...]
    copy = pltpu.make_async_copy(block, shares, sems.at[0])
    copy.start()
    rows = field.shape[1]
    own = rows - 2 * HALO
    fill_adjoint(lam, FLAT, {0: mine})
    for t in tiles(rows):
        s, label = field[Q, t, :], field[Q + 1, t, :]
        rho, u, speed = stored(field, t)
        rate, keep, gain = rates(s, label)
        inlet = label == 3.0
        here = {q: jnp.where(inlet, 0.0, lam[q, t, :]) for q in FLAT}
        by_rho, by_mom, _ = by_moments(here, FLAT, u, speed)
        g0 = gain * by_rho
        gm = [gain * by_mom[a] for a in range(2)]
        near[0, t, :] = g0
        near[1, t, :] = gm[0]
        near[2, t, :] = gm[1]
        out = spread(here, FLAT, s, keep, g0, gm + [None])
        free = 1.0 - s
        two = [2.0 * free * u[a] for a in range(3)]
        less = free * speed
        for i, q in enumerate(FLAT):
            adj[i, t, :] = energy_part(q, out[q], two, less)
    for i, q in enumerate(FLAT):
        flat[i] = shifted(adj[i], -VEL[q][0], -VEL[q][1])[:own]
    copy.wait()


def kernel_four(odd_p, field, mine, pair, other, kinetic, near, late, to_pair, to_other, lam, adj):
    rows = field.shape[1]
    own = rows - 2 * HALO
    odd = odd_p[0] == 1
    low = [pick(odd, other[k], pair[k]) for k in range(3)]
    high = [pick(odd, pair[k], other[k]) for k in range(3)]
    fill_adjoint(lam, range(Q), {0: mine, 1: high, -1: low})
    for t in tiles(rows):
        s = field[Q, t, :]
        out, by_s, rho, u, speed, through = pull_back(
            [lam[q, t, :] for q in range(Q)],
            [field[q, t, :] for q in range(Q)],
            s,
            field[Q + 1, t, :],
            sorted(RISE + FALL),
            stored(field, t),
        )
        free = 1.0 - s
        two = [2.0 * free * u[a] for a in range(3)]
        less = free * speed
        for q in RISE + FALL:
            adj[q, t, :] = energy_part(q, out[q], two, less)
        for k in range(3):
            late[k, t, :] = through[k] - near[k, t, :]
        if t.start < own:
            late[3, t, :] = by_s - rho * speed - kinetic[t, :]
        else:
            late[3, t, :] = jnp.zeros_like(s)

    def pulled(q):
        return shifted(adj[q], -VEL[q][0], -VEL[q][1])[:own]

    for i in range(len(RISE)):
        write_pair(odd, to_pair.at[i], to_other.at[i], pulled(FALL[i]), pulled(RISE[i]))


def kernel_five(cells, odd_z, pop, cell, flat, late, pair, other, energy, sens_h, out_h, sens, out, level, sems):
    own = pop.shape[1]
    odd = odd_z[0] == 1
    copies = []
    for i, q in enumerate(FLAT):
        cx, cy, _ = VEL[q]
        value = late[0]
        if cx:
            value = value + late[1] if cx > 0 else value - late[1]
        if cy:
            value = value + late[2] if cy > 0 else value - late[2]
        level[i] = flat[i] + shifted(value, -cx, -cy)[:own]
    scale = cells / jnp.sum(jnp.sum(energy[...], axis=0), keepdims=True)
    scale = jnp.broadcast_to(scale, (8, pop.shape[2]))
    for t in tiles(own):
        s, label = cell[0, t, :], cell[1, t, :]
        lam = []
        for q in range(Q):
            if VEL[q][2] == 0:
                lam.append(level[FLAT.index(q), t, :])
            elif VEL[q][2] == 1:
                i = RISE.index(q)
                lam.append(pick(odd, pair[i, t, :], other[i, t, :]))
            else:
                i = FALL.index(q)
                lam.append(pick(odd, other[i, t, :], pair[i, t, :]))
        grads, by_s, _, _, _, _ = pull_back(lam, [pop[q, t, :] for q in range(Q)], s, label, range(Q))
        for q in range(Q):
            out[q, t, :] = grads[q] * scale
        sens[t, :] = jnp.where(label == 1.0, (by_s + late[3, t, :]) * scale, 0.0)
        n = t.start // 8
        copies.append(pltpu.make_async_copy(out.at[:, t, :], out_h.at[:, t, :], sems.at[n]))
        copies[-1].start()
    copies.append(pltpu.make_async_copy(sens, sens_h, sems.at[own // 8]))
    copies[-1].start()
    for c in copies:
        c.wait()


def call(kernel, shapes, scratch, flags, *args, hbm_out=0, sems=0, aliases=None):
    fast = pl.BlockSpec(memory_space=pltpu.VMEM)
    slow = pl.BlockSpec(memory_space=pltpu.HBM)
    return pl.pallas_call(
        kernel,
        out_shape=[jax.ShapeDtypeStruct(s, jnp.float32) for s in shapes],
        in_specs=[pl.BlockSpec(memory_space=pltpu.SMEM)] * len(flags)
        + [fast] * len(args),
        out_specs=[fast] * (len(shapes) - hbm_out) + [slow] * hbm_out,
        scratch_shapes=[pltpu.VMEM(s, jnp.float32) for s in scratch]
        + ([pltpu.SemaphoreType.DMA((sems,))] if sems else []),
        input_output_aliases=aliases or {},
        compiler_params=pltpu.CompilerParams(vmem_limit_bytes=16 * 1024 * 1024),
    )(*flags, *args)


class Layout:
    def __init__(self, planes, chunks):
        self.planes, self.chunks = planes, chunks
        self.bricks = [(p, k) for p in range(planes) for k in range(chunks)]
        self.swapped = planes % 2 == 0 and chunks % 2 == 0

    def start(self, p, k):
        return (p % self.planes) * self.chunks + k % self.chunks

    def home(self, p, k):
        p, k = p % self.planes, k % self.chunks
        if not self.swapped:
            return self.start(p, k)
        return self.start(p - p % 2 + (k + ALPHA) % 2, k - k % 2 + (p + BETA) % 2)

    def moves(self, source, target):
        side = lambda p: 1 - 2 * (p % 2)
        still = [(source(p, k), target(p, k)) for p, k in self.bricks]
        pair = [(source(p, k), target(p + side(p), k)) for p, k in self.bricks]
        other = [(source(p, k), target(p - side(p), k)) for p, k in self.bricks]
        return still, pair, other


def on_device(populations, solid_fraction, labels):
    _, _, own, wide = populations.shape
    rows = own + 2 * HALO
    axes = ("gz", "gy")
    planes, chunks = lax.axis_size("gz"), lax.axis_size("gy")
    layout = Layout(planes, chunks)
    flag = lambda axis: (lax.axis_index(axis) % 2).astype(jnp.int32).reshape(1)
    odd_z, odd_y = flag("gz"), flag("gy")
    odd_p = (odd_y + BETA) % 2 if layout.swapped else odd_z
    pop = populations.reshape(Q, own, wide)
    frac = solid_fraction.reshape(own, wide)
    lab = labels.reshape(own, wide)
    whole = lambda n: (n, rows, wide)
    less = lambda n: (n, own, wide)
    edge = lambda n: (n, 2 * HALO, wide)

    marks = lax.optimization_barrier(lab.astype(jnp.float32))
    mixed = jnp.where(marks == 1.0, frac, jnp.where(marks == 2.0, jnp.float32(1.0), jnp.float32(0.0)))
    cell = jnp.stack([mixed, marks])
    size = edge_slots(True)[1]
    edge_a, edge_b, mid, pair, other = call(
        kernel_one,
        [(size, wide)] * 2 + [less(11), whole(5), whole(5)],
        [less(Q)],
        [odd_z, odd_y],
        pop,
        cell,
    )
    side = lambda k: 1 - 2 * (k % 2)
    edge_a = lax.ppermute(edge_a, "gy", [(k, (k + side(k)) % chunks) for k in range(chunks)])
    edge_b = lax.ppermute(edge_b, "gy", [(k, (k - side(k)) % chunks) for k in range(chunks)])
    still_p, pair_p, other_p = layout.moves(layout.start, layout.home)
    mid = lax.ppermute(mid, axes, still_p)
    mid_e, pair, other = call(
        kernel_edge,
        [edge(11), whole(5), whole(5)],
        [],
        [odd_z, odd_y],
        edge_a,
        edge_b,
        pair,
        other,
        aliases={4: 1, 5: 2},
    )
    mid_e = lax.ppermute(mid_e, axes, still_p)
    other = lax.ppermute(other, axes, other_p)
    pair = lax.ppermute(pair, axes, pair_p)
    field, mom, pair, other, part = call(
        kernel_two,
        [whole(Q + 7), whole(3), whole(3), whole(3), (8, wide)],
        [(rows, wide), whole(Q)],
        [odd_p],
        mid,
        pair,
        other,
        mid_e,
    )
    _, pair_p, other_p = layout.moves(layout.home, layout.home)
    other = lax.ppermute(other, axes, other_p)
    pair = lax.ppermute(pair, axes, pair_p)
    mine, pair, other, kinetic, energy = call(
        kernel_three,
        [whole(3), whole(3), whole(3), (own, wide), (8, wide // 2)],
        [],
        [odd_p],
        mom,
        pair,
        other,
        field,
        part,
    )
    other = lax.ppermute(other, axes, other_p)
    pair = lax.ppermute(pair, axes, pair_p)
    count = planes * chunks
    flat, near, energy = call(
        kernel_near,
        [less(9), whole(3), (count, 8, wide // 2)],
        [whole(Q), whole(9), (count, 8, wide // 2)],
        [],
        field,
        mine,
        energy,
        hbm_out=1,
        sems=1,
    )
    energy = lax.all_to_all(energy, axes, 0, 0, tiled=True)
    late, pair, other = call(
        kernel_four,
        [whole(4), less(5), less(5)],
        [whole(Q), whole(Q)],
        [odd_p],
        field,
        mine,
        pair,
        other,
        kinetic,
        near,
    )
    still_p, pair_p, other_p = layout.moves(layout.home, layout.start)
    flat = lax.ppermute(flat, axes, still_p)
    pair = lax.ppermute(pair, axes, pair_p)
    other = lax.ppermute(other, axes, other_p)
    late = lax.ppermute(late, axes, still_p)
    cells = float(STEPS * own * wide * populations.shape[1] * planes * chunks)
    sens, out = call(
        functools.partial(kernel_five, cells),
        [(own, wide), less(Q)],
        [(own, wide), less(Q), less(9)],
        [odd_z],
        pop,
        cell,
        flat,
        late,
        pair,
        other,
        energy,
        hbm_out=2,
        sems=own // 8 + 1,
    )
    return sens.reshape(solid_fraction.shape), out.reshape(populations.shape)


def solution(mesh):
    in_specs = (P(None, "gz", "gy", None), P("gz", "gy", None), P("gz", "gy", None))
    out_specs = (P("gz", "gy", None), P(None, "gz", "gy", None))
    return jax.shard_map(on_device, mesh=mesh, in_specs=in_specs, out_specs=out_specs, check_vma=False)
```

```python
import functools

import jax
import jax.numpy as jnp
from jax import lax
from jax.experimental import pallas as pl
from jax.experimental.pallas import tpu as pltpu
from jax.sharding import PartitionSpec as P

STEPS = 2
OMEGA = 0.9
INLET_SPEED = 0.05
HALO = 4
ALPHA, BETA = 0, 1


def velocity_table():
    velocities = [(0, 0, 0)]
    for axis in range(3):
        for sign in (1, -1):
            vector = [0, 0, 0]
            vector[axis] = sign
            velocities.append(tuple(vector))
    for first in range(3):
        for second in range(first + 1, 3):
            for sign_a in (1, -1):
                for sign_b in (1, -1):
                    vector = [0, 0, 0]
                    vector[first] = sign_a
                    vector[second] = sign_b
                    velocities.append(tuple(vector))
    weights = [1.0 / 3.0] + [1.0 / 18.0] * 6 + [1.0 / 36.0] * 12
    opposite = [velocities.index(tuple((-e for e in vector))) for vector in velocities]
    return (velocities, weights, opposite)


VEL, WEIGHT, OPP = velocity_table()
Q = len(VEL)
FLAT = [q for q in range(Q) if VEL[q][2] == 0]
RISE = [q for q in range(Q) if VEL[q][2] == 1]
FALL = [q for q in range(Q) if VEL[q][2] == -1]


def inlet_value(q):
    along = VEL[q][2] * INLET_SPEED
    return WEIGHT[q] * (1.0 + 3.0 * along + 4.5 * along * along - 1.5 * INLET_SPEED * INLET_SPEED)


def signed_sum(terms):
    total = None
    for sign, term in terms:
        if total is None:
            total = term if sign > 0 else -term
        else:
            total = total + term if sign > 0 else total - term
    return total


def first_moments(f):
    out = []
    for axis in range(3):
        out.append(signed_sum(sorted(((VEL[q][axis], f[q]) for q in range(Q) if VEL[q][axis]), key=lambda t: -t[0])))
    return out


def dot_c(q, vector):
    return signed_sum(sorted(((VEL[q][a], vector[a]) for a in range(3) if VEL[q][a]), key=lambda t: -t[0]))


def macroscopic(f):
    rho = functools.reduce(lambda a, b: a + b, f)
    mom = first_moments(f)
    inv = 1.0 / rho
    u = [m * inv for m in mom]
    speed = u[0] * u[0] + u[1] * u[1] + u[2] * u[2]
    return rho, u, speed


def collide(f, s, lab):
    rho, u, speed = macroscopic(f)
    rate = jnp.where(lab == 4.0, 1.0, OMEGA)
    inlet = lab == 3.0
    free = 1.0 - s
    keep = free * (1.0 - rate)
    gain = free * rate * rho
    base = 1.0 - 1.5 * speed
    post = [None] * Q
    for q in range(Q):
        o = OPP[q]
        if o < q:
            continue
        scaled = gain * WEIGHT[q]
        if q == 0:
            post[0] = (keep + s) * f[0] + scaled * base
            continue
        along = dot_c(q, u)
        even = scaled * (base + 4.5 * along * along)
        odd = scaled * (3.0 * along)
        post[q] = keep * f[q] + s * f[o] + (even + odd)
        post[o] = keep * f[o] + s * f[q] + (even - odd)
    return [jnp.where(inlet, inlet_value(q), post[q]) for q in range(Q)], rho, u, speed


def total(terms):
    return functools.reduce(lambda a, b: a + b, terms)


def by_moments(lam, group, u, speed):
    near = [q for q in group if 0 < q < 7]
    far = [q for q in group if q >= 7]

    def weighted(sign):
        out = None
        for weight, part in ((WEIGHT[1], near), (WEIGHT[7], far)):
            terms = sorted(((sign(VEL[q]), lam[q]) for q in part if sign(VEL[q])), key=lambda t: -t[0])
            if terms:
                term = weight * signed_sum(terms)
                out = term if out is None else out + term
        return out

    s0 = weighted(lambda c: 1)
    if 0 in group:
        s0 = s0 + WEIGHT[0] * lam[0]
    s1 = [weighted(lambda c: c[a]) for a in range(3)]
    tens = {(a, b): weighted(lambda c: c[a] * c[b]) for a in range(3) for b in range(3)}
    plus = lambda terms: total(terms) if terms else None
    tu = [plus([tens[a, b] * u[b] for b in range(3) if tens[a, b] is not None]) for a in range(3)]
    utu = total([tu[a] * u[a] for a in range(3) if tu[a] is not None])
    by_rho = s0 * (1.0 + 1.5 * speed) - 4.5 * utu
    by_mom = []
    for a in range(3):
        value = -3.0 * u[a] * s0
        if tu[a] is not None:
            value = value + 9.0 * tu[a]
        if s1[a] is not None:
            value = value + 3.0 * s1[a]
        by_mom.append(value)
    s1u = total([s1[a] * u[a] for a in range(3) if s1[a] is not None])
    along = s0 * (1.0 - 1.5 * speed) + 3.0 * s1u + 4.5 * utu
    return by_rho, by_mom, along


def stored(field, t, c):
    return field[Q + 2, t, c], [field[Q + 3 + a, t, c] for a in range(3)], field[Q + 6, t, c]


def rates(s, lab):
    rate = jnp.where(lab == 4.0, 1.0, OMEGA)
    free = 1.0 - s
    return rate, free * (1.0 - rate), free * rate


def spread(lam, group, s, keep, g0, gm):
    out = {}
    for q in group:
        o = OPP[q]
        if q == 0:
            out[0] = (keep + s) * lam[0] + g0
        elif q < o:
            along = dot_c(q, gm)
            out[q] = keep * lam[q] + s * lam[o] + (g0 + along)
            out[o] = keep * lam[o] + s * lam[q] + (g0 - along)
    return out


def pull_back(lam, f, s, lab, group, known=None):
    rho, u, speed = known or macroscopic(f)
    rate, keep, gain = rates(s, lab)
    inlet = lab == 3.0
    lam = [jnp.where(inlet, 0.0, v) for v in lam]
    by_rho, by_mom, along = by_moments(lam, range(Q), u, speed)
    g0 = gain * by_rho
    gm = [gain * by_mom[a] for a in range(3)]
    out = spread(lam, group, s, keep, g0, gm)
    bounce = lam[0] * f[0]
    plain = lam[0] * f[0]
    for q in range(1, Q):
        o = OPP[q]
        if q < o:
            bounce = bounce + (lam[q] * f[o] + lam[o] * f[q])
            plain = plain + (lam[q] * f[q] + lam[o] * f[o])
    by_s = bounce - (1.0 - rate) * plain - rate * (rho * along)
    return out, by_s, rho, u, speed, (g0, gm[0], gm[1])


def shifted(value, dx, dy):
    if dx:
        value = pltpu.roll(value, dx % value.shape[1], 1)
    if dy:
        value = pltpu.roll(value, dy % value.shape[0], 0)
    return value


def tiles(rows, wide):
    half = wide // 2
    return [(pl.ds(8 * t, 8), pl.ds(half * k, half)) for t in range(rows // 8) for k in range(2)]


def pick(odd, first, second):
    return jnp.where(odd, second, first)


def write_pair(odd, to_pair, to_other, rising, falling):
    to_pair[...] = pick(odd, rising, falling)
    to_other[...] = pick(odd, falling, rising)


def edge_rows(q, high):
    if q >= Q:
        return HALO - 1
    cy = VEL[q][1] if high else -VEL[q][1]
    return {0: HALO - 1, 1: HALO - 2, -1: HALO}[cy]


def edge_slots(high):
    slots, at = {}, 0
    for q in range(Q + 2):
        n = edge_rows(q, high)
        slots[q] = (at, n)
        at += n
    return slots, at


def kernel_one(odd_z, odd_y, pop, cell, edge_pair, edge_other, mid, pair, other, post):
    own = pop.shape[1]
    odd, oy = odd_z[0] == 1, odd_y[0] == 1
    for t, c in tiles(own, pop.shape[2]):
        s, label = cell[0, t, c], cell[1, t, c]
        out, _, _, _ = collide([pop[q, t, c] for q in range(Q)], s, label)
        for q in range(Q):
            post[q, t, c] = out[q]
        mid[len(FLAT), t, c] = s
        mid[len(FLAT) + 1, t, c] = label
    for q in range(Q):
        if VEL[q][0]:
            post[q] = shifted(post[q], VEL[q][0], 0)
    low_slots, size = edge_slots(True)
    high_slots, _ = edge_slots(False)
    field = lambda q: post.at[q] if q < Q else cell.at[q - Q]

    def fill(to_high, to_low):
        for q in range(Q + 2):
            at, n = low_slots[q]
            to_low[at : at + n, :] = field(q)[:n, :]
            at, n = high_slots[q]
            to_high[at : at + n, :] = field(q)[own - n : own, :]

    @pl.when(oy)
    def _():
        fill(edge_other, edge_pair)

    @pl.when(jnp.logical_not(oy))
    def _():
        fill(edge_pair, edge_other)

    for i, q in enumerate(FLAT):
        mid[i] = post[q]
    for i in range(len(RISE)):
        for t, c in tiles(own, pop.shape[2]):
            write_pair(odd, pair.at[i, t, c], other.at[i, t, c], post[RISE[i], t, c], post[FALL[i], t, c])


def kernel_edge(odd_z, odd_y, edge_pair, edge_other, pair_in, other_in, mid, pair, other):
    rows = pair.shape[1]
    odd, oy = odd_z[0] == 1, odd_y[0] == 1
    from_high, size = edge_slots(True)
    from_low, _ = edge_slots(False)
    zeros = lambda n: [jnp.zeros((n, pair.shape[2]), jnp.float32)] if n else []

    def tile(q, high, low):
        at, n = from_high[q]
        top = [high[at : at + n, :]] + zeros(HALO - n)
        at, n = from_low[q]
        return jnp.concatenate(top + zeros(HALO - n) + [low[at : at + n, :]], axis=0)

    def build(high, low):
        for i, q in enumerate(FLAT + [Q, Q + 1]):
            mid[i] = tile(q, high, low)
        r = pl.ds(rows - 2 * HALO, 2 * HALO)
        for i in range(len(RISE)):
            write_pair(odd, pair.at[i, r, :], other.at[i, r, :], tile(RISE[i], high, low), tile(FALL[i], high, low))

    @pl.when(oy)
    def _():
        build(edge_other, edge_pair)

    @pl.when(jnp.logical_not(oy))
    def _():
        build(edge_pair, edge_other)


def kernel_two(odd_p, mid, pair, other, mid_e, field, mom, to_pair, to_other, part, raw, post):
    rows = field.shape[1]
    own = rows - 2 * HALO
    odd = odd_p[0] == 1
    for q in range(Q):
        cz = VEL[q][2]
        if cz == 0:
            raw[:own, :] = mid[FLAT.index(q)]
            raw[own:, :] = mid_e[FLAT.index(q)]
            value = raw[...]
        elif cz == 1:
            i = RISE.index(q)
            value = pick(odd, other[i], pair[i])
        else:
            i = FALL.index(q)
            value = pick(odd, pair[i], other[i])
        field[q] = shifted(value, 0, VEL[q][1])
    for i in (0, 1):
        field[Q + i, :own, :] = mid[len(FLAT) + i]
        field[Q + i, own:, :] = mid_e[len(FLAT) + i]
    total = None
    for t, c in tiles(rows, field.shape[2]):
        s = field[Q, t, c]
        out, rho, u, speed = collide([field[q, t, c] for q in range(Q)], s, field[Q + 1, t, c])
        for q in range(Q):
            post[q, t, c] = out[q]
        for i, value in enumerate([rho] + u + [speed]):
            field[Q + 2 + i, t, c] = value
        if t.start < own:
            e = (1.0 - s) * (rho * speed)
            total = e if total is None else total + e
    part[...] = total
    results = []
    for group in (FLAT, RISE, FALL):
        sums = [None, None, None]
        for q in group:
            cx, cy, _ = VEL[q]
            v = shifted(post[q], cx, cy)
            for k, sign in ((0, 1), (1, cx), (2, cy)):
                if sign:
                    if sums[k] is None:
                        sums[k] = v if sign > 0 else -v
                    else:
                        sums[k] = sums[k] + v if sign > 0 else sums[k] - v
        results.append(sums)
    for k in range(3):
        mom[k] = results[0][k]
        write_pair(odd, to_pair.at[k], to_other.at[k], results[1][k], results[2][k])


def kernel_three(odd_p, mom, pair, other, field, part, mine, to_pair, to_other, kinetic, out):
    rows = mom.shape[1]
    own = rows - 2 * HALO
    odd = odd_p[0] == 1
    total = part[...]
    for t, c in tiles(rows, field.shape[2]):
        below = [pick(odd, other[k, t, c], pair[k, t, c]) for k in range(3)]
        above = [pick(odd, pair[k, t, c], other[k, t, c]) for k in range(3)]
        rho = mom[0, t, c] + below[0] + above[0]
        inv = 1.0 / rho
        ux = (mom[1, t, c] + below[1] + above[1]) * inv
        uy = (mom[2, t, c] + below[2] + above[2]) * inv
        uz = (below[0] - above[0]) * inv
        speed = ux * ux + uy * uy + uz * uz
        free = 1.0 - field[Q, t, c]
        two = 2.0 * free
        ax, ay, az, b = two * ux, two * uy, two * uz, free * speed
        mine[0, t, c] = ax
        mine[1, t, c] = ay
        mine[2, t, c] = b
        to_pair[0, t, c] = ax
        to_pair[1, t, c] = ay
        to_other[0, t, c] = ax
        to_other[1, t, c] = ay
        write_pair(odd, to_pair.at[2, t, c], to_other.at[2, t, c], -az - b, az - b)
        if t.start < own:
            k = rho * speed
            kinetic[t, c] = k
            total = total + free * k
    out[...] = total


def fill_adjoint(lam, group, sources):
    for q in group:
        cx, cy, cz = VEL[q]
        ref = sources[cz]
        value = ref[2]
        if cz == 0:
            value = -value
        if cx:
            value = value + ref[0] if cx > 0 else value - ref[0]
        if cy:
            value = value + ref[1] if cy > 0 else value - ref[1]
        lam[q] = shifted(value, -cx, -cy)


def energy_part(q, out, two, less):
    e = out - less
    return e + dot_c(q, two) if q else e


def kernel_near(field, mine, energy, flat, near, shares, lam, adj, block, sems):
    for i in range(block.shape[0]):
        block[i] = energy[...]
    copy = pltpu.make_async_copy(block, shares, sems.at[0])
    copy.start()
    rows = field.shape[1]
    own = rows - 2 * HALO
    fill_adjoint(lam, FLAT, {0: mine})
    for t, c in tiles(rows, field.shape[2]):
        s, label = field[Q, t, c], field[Q + 1, t, c]
        rho, u, speed = stored(field, t, c)
        rate, keep, gain = rates(s, label)
        inlet = label == 3.0
        here = {q: jnp.where(inlet, 0.0, lam[q, t, c]) for q in FLAT}
        by_rho, by_mom, _ = by_moments(here, FLAT, u, speed)
        g0 = gain * by_rho
        gm = [gain * by_mom[a] for a in range(2)]
        near[0, t, c] = g0
        near[1, t, c] = gm[0]
        near[2, t, c] = gm[1]
        out = spread(here, FLAT, s, keep, g0, gm + [None])
        free = 1.0 - s
        two = [2.0 * free * u[a] for a in range(3)]
        less = free * speed
        for i, q in enumerate(FLAT):
            adj[i, t, c] = energy_part(q, out[q], two, less)
    for i, q in enumerate(FLAT):
        flat[i] = shifted(adj[i], -VEL[q][0], -VEL[q][1])[:own]
    copy.wait()


def kernel_four(odd_p, field, mine, pair, other, kinetic, near, late, to_pair, to_other, lam, adj):
    rows = field.shape[1]
    own = rows - 2 * HALO
    odd = odd_p[0] == 1
    low = [pick(odd, other[k], pair[k]) for k in range(3)]
    high = [pick(odd, pair[k], other[k]) for k in range(3)]
    fill_adjoint(lam, range(Q), {0: mine, 1: high, -1: low})
    for t, c in tiles(rows, field.shape[2]):
        s = field[Q, t, c]
        out, by_s, rho, u, speed, through = pull_back(
            [lam[q, t, c] for q in range(Q)],
            [field[q, t, c] for q in range(Q)],
            s,
            field[Q + 1, t, c],
            sorted(RISE + FALL),
            stored(field, t, c),
        )
        free = 1.0 - s
        two = [2.0 * free * u[a] for a in range(3)]
        less = free * speed
        for q in RISE + FALL:
            adj[q, t, c] = energy_part(q, out[q], two, less)
        for k in range(3):
            late[k, t, c] = through[k] - near[k, t, c]
        if t.start < own:
            late[3, t, c] = by_s - rho * speed - kinetic[t, c]
        else:
            late[3, t, c] = jnp.zeros_like(s)

    def pulled(q):
        return shifted(adj[q], -VEL[q][0], -VEL[q][1])[:own]

    for i in range(len(RISE)):
        write_pair(odd, to_pair.at[i], to_other.at[i], pulled(FALL[i]), pulled(RISE[i]))


def kernel_five(cells, odd_z, pop, cell, flat, late, pair, other, energy, sens_h, out_h, sens, out, level, sems):
    own = pop.shape[1]
    odd = odd_z[0] == 1
    copies = []
    for i, q in enumerate(FLAT):
        cx, cy, _ = VEL[q]
        value = late[0]
        if cx:
            value = value + late[1] if cx > 0 else value - late[1]
        if cy:
            value = value + late[2] if cy > 0 else value - late[2]
        level[i] = flat[i] + shifted(value, -cx, -cy)[:own]
    scale = cells / jnp.sum(jnp.sum(energy[...], axis=0), keepdims=True)
    scale = jnp.broadcast_to(scale, (8, pop.shape[2] // 2))
    for t, c in tiles(own, pop.shape[2]):
        s, label = cell[0, t, c], cell[1, t, c]
        lam = []
        for q in range(Q):
            if VEL[q][2] == 0:
                lam.append(level[FLAT.index(q), t, c])
            elif VEL[q][2] == 1:
                i = RISE.index(q)
                lam.append(pick(odd, pair[i, t, c], other[i, t, c]))
            else:
                i = FALL.index(q)
                lam.append(pick(odd, other[i, t, c], pair[i, t, c]))
        grads, by_s, _, _, _, _ = pull_back(lam, [pop[q, t, c] for q in range(Q)], s, label, range(Q))
        for q in range(Q):
            out[q, t, c] = grads[q] * scale
        sens[t, c] = jnp.where(label == 1.0, (by_s + late[3, t, c]) * scale, 0.0)
        n = len(copies)
        copies.append(pltpu.make_async_copy(out.at[:, t, c], out_h.at[:, t, c], sems.at[n]))
        copies[-1].start()
    copies.append(pltpu.make_async_copy(sens, sens_h, sems.at[own // 4]))
    copies[-1].start()
    for c in copies:
        c.wait()


def call(kernel, shapes, scratch, flags, *args, hbm_out=0, sems=0, aliases=None):
    fast = pl.BlockSpec(memory_space=pltpu.VMEM)
    slow = pl.BlockSpec(memory_space=pltpu.HBM)
    return pl.pallas_call(
        kernel,
        out_shape=[jax.ShapeDtypeStruct(s, jnp.float32) for s in shapes],
        in_specs=[pl.BlockSpec(memory_space=pltpu.SMEM)] * len(flags)
        + [fast] * len(args),
        out_specs=[fast] * (len(shapes) - hbm_out) + [slow] * hbm_out,
        scratch_shapes=[pltpu.VMEM(s, jnp.float32) for s in scratch]
        + ([pltpu.SemaphoreType.DMA((sems,))] if sems else []),
        input_output_aliases=aliases or {},
        compiler_params=pltpu.CompilerParams(vmem_limit_bytes=16 * 1024 * 1024),
    )(*flags, *args)


class Layout:
    def __init__(self, planes, chunks):
        self.planes, self.chunks = planes, chunks
        self.bricks = [(p, k) for p in range(planes) for k in range(chunks)]
        self.swapped = planes % 2 == 0 and chunks % 2 == 0

    def start(self, p, k):
        return (p % self.planes) * self.chunks + k % self.chunks

    def home(self, p, k):
        p, k = p % self.planes, k % self.chunks
        if not self.swapped:
            return self.start(p, k)
        return self.start(p - p % 2 + (k + ALPHA) % 2, k - k % 2 + (p + BETA) % 2)

    def moves(self, source, target):
        side = lambda p: 1 - 2 * (p % 2)
        still = [(source(p, k), target(p, k)) for p, k in self.bricks]
        pair = [(source(p, k), target(p + side(p), k)) for p, k in self.bricks]
        other = [(source(p, k), target(p - side(p), k)) for p, k in self.bricks]
        return still, pair, other


def on_device(populations, solid_fraction, labels):
    _, _, own, wide = populations.shape
    rows = own + 2 * HALO
    axes = ("gz", "gy")
    planes, chunks = lax.axis_size("gz"), lax.axis_size("gy")
    layout = Layout(planes, chunks)
    flag = lambda axis: (lax.axis_index(axis) % 2).astype(jnp.int32).reshape(1)
    odd_z, odd_y = flag("gz"), flag("gy")
    odd_p = (odd_y + BETA) % 2 if layout.swapped else odd_z
    pop = populations.reshape(Q, own, wide)
    frac = solid_fraction.reshape(own, wide)
    lab = labels.reshape(own, wide)
    whole = lambda n: (n, rows, wide)
    less = lambda n: (n, own, wide)
    edge = lambda n: (n, 2 * HALO, wide)

    marks = lax.optimization_barrier(lab.astype(jnp.float32))
    mixed = jnp.where(marks == 1.0, frac, jnp.where(marks == 2.0, jnp.float32(1.0), jnp.float32(0.0)))
    cell = jnp.stack([mixed, marks])
    size = edge_slots(True)[1]
    edge_a, edge_b, mid, pair, other = call(
        kernel_one,
        [(size, wide)] * 2 + [less(11), whole(5), whole(5)],
        [less(Q)],
        [odd_z, odd_y],
        pop,
        cell,
    )
    side = lambda k: 1 - 2 * (k % 2)
    edge_a = lax.ppermute(edge_a, "gy", [(k, (k + side(k)) % chunks) for k in range(chunks)])
    edge_b = lax.ppermute(edge_b, "gy", [(k, (k - side(k)) % chunks) for k in range(chunks)])
    still_p, pair_p, other_p = layout.moves(layout.start, layout.home)
    mid = lax.ppermute(mid, axes, still_p)
    mid_e, pair, other = call(
        kernel_edge,
        [edge(11), whole(5), whole(5)],
        [],
        [odd_z, odd_y],
        edge_a,
        edge_b,
        pair,
        other,
        aliases={4: 1, 5: 2},
    )
    mid_e = lax.ppermute(mid_e, axes, still_p)
    other = lax.ppermute(other, axes, other_p)
    pair = lax.ppermute(pair, axes, pair_p)
    field, mom, pair, other, part = call(
        kernel_two,
        [whole(Q + 7), whole(3), whole(3), whole(3), (8, wide // 2)],
        [(rows, wide), whole(Q)],
        [odd_p],
        mid,
        pair,
        other,
        mid_e,
    )
    _, pair_p, other_p = layout.moves(layout.home, layout.home)
    other = lax.ppermute(other, axes, other_p)
    pair = lax.ppermute(pair, axes, pair_p)
    mine, pair, other, kinetic, energy = call(
        kernel_three,
        [whole(3), whole(3), whole(3), (own, wide), (8, wide // 2)],
        [],
        [odd_p],
        mom,
        pair,
        other,
        field,
        part,
    )
    other = lax.ppermute(other, axes, other_p)
    pair = lax.ppermute(pair, axes, pair_p)
    count = planes * chunks
    flat, near, energy = call(
        kernel_near,
        [less(9), whole(3), (count, 8, wide // 2)],
        [whole(Q), whole(9), (count, 8, wide // 2)],
        [],
        field,
        mine,
        energy,
        hbm_out=1,
        sems=1,
    )
    energy = lax.all_to_all(energy, axes, 0, 0, tiled=True)
    late, pair, other = call(
        kernel_four,
        [whole(4), less(5), less(5)],
        [whole(Q), whole(Q)],
        [odd_p],
        field,
        mine,
        pair,
        other,
        kinetic,
        near,
    )
    still_p, pair_p, other_p = layout.moves(layout.home, layout.start)
    flat = lax.ppermute(flat, axes, still_p)
    pair = lax.ppermute(pair, axes, pair_p)
    other = lax.ppermute(other, axes, other_p)
    late = lax.ppermute(late, axes, still_p)
    cells = float(STEPS * own * wide * populations.shape[1] * planes * chunks)
    sens, out = call(
        functools.partial(kernel_five, cells),
        [(own, wide), less(Q)],
        [(own, wide), less(Q), less(9)],
        [odd_z],
        pop,
        cell,
        flat,
        late,
        pair,
        other,
        energy,
        hbm_out=2,
        sems=own // 4 + 1,
    )
    return sens.reshape(solid_fraction.shape), out.reshape(populations.shape)


def solution(mesh):
    in_specs = (P(None, "gz", "gy", None), P("gz", "gy", None), P("gz", "gy", None))
    out_specs = (P("gz", "gy", None), P(None, "gz", "gy", None))
    return jax.shard_map(on_device, mesh=mesh, in_specs=in_specs, out_specs=out_specs, check_vma=False)
```

```python
import functools

import jax
import jax.numpy as jnp
from jax import lax
from jax.experimental import pallas as pl
from jax.experimental.pallas import tpu as pltpu
from jax.sharding import PartitionSpec as P

STEPS = 2
OMEGA = 0.9
INLET_SPEED = 0.05
HALO = 4
ALPHA, BETA = 0, 1


def velocity_table():
    velocities = [(0, 0, 0)]
    for axis in range(3):
        for sign in (1, -1):
            vector = [0, 0, 0]
            vector[axis] = sign
            velocities.append(tuple(vector))
    for first in range(3):
        for second in range(first + 1, 3):
            for sign_a in (1, -1):
                for sign_b in (1, -1):
                    vector = [0, 0, 0]
                    vector[first] = sign_a
                    vector[second] = sign_b
                    velocities.append(tuple(vector))
    weights = [1.0 / 3.0] + [1.0 / 18.0] * 6 + [1.0 / 36.0] * 12
    opposite = [velocities.index(tuple((-e for e in vector))) for vector in velocities]
    return (velocities, weights, opposite)


VEL, WEIGHT, OPP = velocity_table()
Q = len(VEL)
FLAT = [q for q in range(Q) if VEL[q][2] == 0]
RISE = [q for q in range(Q) if VEL[q][2] == 1]
FALL = [q for q in range(Q) if VEL[q][2] == -1]


def inlet_value(q):
    along = VEL[q][2] * INLET_SPEED
    return WEIGHT[q] * (1.0 + 3.0 * along + 4.5 * along * along - 1.5 * INLET_SPEED * INLET_SPEED)


def signed_sum(terms):
    total = None
    for sign, term in terms:
        if total is None:
            total = term if sign > 0 else -term
        else:
            total = total + term if sign > 0 else total - term
    return total


def first_moments(f):
    out = []
    for axis in range(3):
        out.append(signed_sum(sorted(((VEL[q][axis], f[q]) for q in range(Q) if VEL[q][axis]), key=lambda t: -t[0])))
    return out


def dot_c(q, vector):
    return signed_sum(sorted(((VEL[q][a], vector[a]) for a in range(3) if VEL[q][a]), key=lambda t: -t[0]))


def macroscopic(f):
    rho = functools.reduce(lambda a, b: a + b, f)
    mom = first_moments(f)
    inv = 1.0 / rho
    u = [m * inv for m in mom]
    speed = u[0] * u[0] + u[1] * u[1] + u[2] * u[2]
    return rho, u, speed


def collide(f, s, lab):
    rho, u, speed = macroscopic(f)
    rate = jnp.where(lab == 4.0, 1.0, OMEGA)
    inlet = lab == 3.0
    free = 1.0 - s
    keep = free * (1.0 - rate)
    gain = free * rate * rho
    base = 1.0 - 1.5 * speed
    post = [None] * Q
    for q in range(Q):
        o = OPP[q]
        if o < q:
            continue
        scaled = gain * WEIGHT[q]
        if q == 0:
            post[0] = (keep + s) * f[0] + scaled * base
            continue
        along = dot_c(q, u)
        even = scaled * (base + 4.5 * along * along)
        odd = scaled * (3.0 * along)
        post[q] = keep * f[q] + s * f[o] + (even + odd)
        post[o] = keep * f[o] + s * f[q] + (even - odd)
    return [jnp.where(inlet, inlet_value(q), post[q]) for q in range(Q)], rho, u, speed


def total(terms):
    return functools.reduce(lambda a, b: a + b, terms)


def by_moments(lam, group, u, speed):
    near = [q for q in group if 0 < q < 7]
    far = [q for q in group if q >= 7]

    def weighted(sign):
        out = None
        for weight, part in ((WEIGHT[1], near), (WEIGHT[7], far)):
            terms = sorted(((sign(VEL[q]), lam[q]) for q in part if sign(VEL[q])), key=lambda t: -t[0])
            if terms:
                term = weight * signed_sum(terms)
                out = term if out is None else out + term
        return out

    s0 = weighted(lambda c: 1)
    if 0 in group:
        s0 = s0 + WEIGHT[0] * lam[0]
    s1 = [weighted(lambda c: c[a]) for a in range(3)]
    tens = {(a, b): weighted(lambda c: c[a] * c[b]) for a in range(3) for b in range(3)}
    plus = lambda terms: total(terms) if terms else None
    tu = [plus([tens[a, b] * u[b] for b in range(3) if tens[a, b] is not None]) for a in range(3)]
    utu = total([tu[a] * u[a] for a in range(3) if tu[a] is not None])
    by_rho = s0 * (1.0 + 1.5 * speed) - 4.5 * utu
    by_mom = []
    for a in range(3):
        value = -3.0 * u[a] * s0
        if tu[a] is not None:
            value = value + 9.0 * tu[a]
        if s1[a] is not None:
            value = value + 3.0 * s1[a]
        by_mom.append(value)
    s1u = total([s1[a] * u[a] for a in range(3) if s1[a] is not None])
    along = s0 * (1.0 - 1.5 * speed) + 3.0 * s1u + 4.5 * utu
    return by_rho, by_mom, along


def stored(field, t, c):
    return field[Q + 2, t, c], [field[Q + 3 + a, t, c] for a in range(3)], field[Q + 6, t, c]


def rates(s, lab):
    rate = jnp.where(lab == 4.0, 1.0, OMEGA)
    free = 1.0 - s
    return rate, free * (1.0 - rate), free * rate


def spread(lam, group, s, keep, g0, gm):
    out = {}
    for q in group:
        o = OPP[q]
        if q == 0:
            out[0] = (keep + s) * lam[0] + g0
        elif q < o:
            along = dot_c(q, gm)
            out[q] = keep * lam[q] + s * lam[o] + (g0 + along)
            out[o] = keep * lam[o] + s * lam[q] + (g0 - along)
    return out


def pull_back(lam, f, s, lab, group, known=None):
    rho, u, speed = known or macroscopic(f)
    rate, keep, gain = rates(s, lab)
    inlet = lab == 3.0
    lam = [jnp.where(inlet, 0.0, v) for v in lam]
    by_rho, by_mom, along = by_moments(lam, range(Q), u, speed)
    g0 = gain * by_rho
    gm = [gain * by_mom[a] for a in range(3)]
    out = spread(lam, group, s, keep, g0, gm)
    bounce = lam[0] * f[0]
    plain = lam[0] * f[0]
    for q in range(1, Q):
        o = OPP[q]
        if q < o:
            bounce = bounce + (lam[q] * f[o] + lam[o] * f[q])
            plain = plain + (lam[q] * f[q] + lam[o] * f[o])
    by_s = bounce - (1.0 - rate) * plain - rate * (rho * along)
    return out, by_s, rho, u, speed, (g0, gm[0], gm[1])


def shifted(value, dx, dy):
    if dx:
        value = pltpu.roll(value, dx % value.shape[1], 1)
    if dy:
        value = pltpu.roll(value, dy % value.shape[0], 0)
    return value


def bands(rows):
    return [pl.ds(8 * t, 8) for t in range(rows // 8)]


def tiles(rows, wide):
    half = wide // 2
    return [(pl.ds(8 * t, 8), pl.ds(half * k, half)) for t in range(rows // 8) for k in range(2)]


def pick(odd, first, second):
    return jnp.where(odd, second, first)


def write_pair(odd, to_pair, to_other, rising, falling):
    to_pair[...] = pick(odd, rising, falling)
    to_other[...] = pick(odd, falling, rising)


def edge_rows(q, high):
    if q >= Q:
        return HALO - 1
    cy = VEL[q][1] if high else -VEL[q][1]
    return {0: HALO - 1, 1: HALO - 2, -1: HALO}[cy]


def edge_slots(high):
    slots, at = {}, 0
    for q in range(Q + 2):
        n = edge_rows(q, high)
        slots[q] = (at, n)
        at += n
    return slots, at


def kernel_one(odd_z, odd_y, pop, cell, edge_pair, edge_other, mid, pair, other, post):
    own = pop.shape[1]
    odd, oy = odd_z[0] == 1, odd_y[0] == 1
    for t in bands(own):
        s, label = cell[0, t, :], cell[1, t, :]
        out, _, _, _ = collide([pop[q, t, :] for q in range(Q)], s, label)
        for q in range(Q):
            post[q, t, :] = shifted(out[q], VEL[q][0], 0)
        mid[len(FLAT), t, :] = s
        mid[len(FLAT) + 1, t, :] = label
    low_slots, size = edge_slots(True)
    high_slots, _ = edge_slots(False)
    field = lambda q: post.at[q] if q < Q else cell.at[q - Q]

    def fill(to_high, to_low):
        for q in range(Q + 2):
            at, n = low_slots[q]
            to_low[at : at + n, :] = field(q)[:n, :]
            at, n = high_slots[q]
            to_high[at : at + n, :] = field(q)[own - n : own, :]

    @pl.when(oy)
    def _():
        fill(edge_other, edge_pair)

    @pl.when(jnp.logical_not(oy))
    def _():
        fill(edge_pair, edge_other)

    for i, q in enumerate(FLAT):
        mid[i] = post[q]
    for i in range(len(RISE)):
        for t in bands(own):
            write_pair(odd, pair.at[i, t, :], other.at[i, t, :], post[RISE[i], t, :], post[FALL[i], t, :])


def kernel_edge(odd_z, odd_y, edge_pair, edge_other, pair_in, other_in, mid, pair, other):
    rows = pair.shape[1]
    odd, oy = odd_z[0] == 1, odd_y[0] == 1
    from_high, size = edge_slots(True)
    from_low, _ = edge_slots(False)
    zeros = lambda n: [jnp.zeros((n, pair.shape[2]), jnp.float32)] if n else []

    def tile(q, high, low):
        at, n = from_high[q]
        top = [high[at : at + n, :]] + zeros(HALO - n)
        at, n = from_low[q]
        return jnp.concatenate(top + zeros(HALO - n) + [low[at : at + n, :]], axis=0)

    def build(high, low):
        for i, q in enumerate(FLAT + [Q, Q + 1]):
            mid[i] = tile(q, high, low)
        r = pl.ds(rows - 2 * HALO, 2 * HALO)
        for i in range(len(RISE)):
            write_pair(odd, pair.at[i, r, :], other.at[i, r, :], tile(RISE[i], high, low), tile(FALL[i], high, low))

    @pl.when(oy)
    def _():
        build(edge_other, edge_pair)

    @pl.when(jnp.logical_not(oy))
    def _():
        build(edge_pair, edge_other)


def kernel_two(odd_p, mid, pair, other, mid_e, field, mom, to_pair, to_other, part, raw, post):
    rows = field.shape[1]
    own = rows - 2 * HALO
    odd = odd_p[0] == 1
    for q in range(Q):
        cz = VEL[q][2]
        if cz == 0:
            raw[:own, :] = mid[FLAT.index(q)]
            raw[own:, :] = mid_e[FLAT.index(q)]
            value = raw[...]
        elif cz == 1:
            i = RISE.index(q)
            value = pick(odd, other[i], pair[i])
        else:
            i = FALL.index(q)
            value = pick(odd, pair[i], other[i])
        field[q] = shifted(value, 0, VEL[q][1])
    for i in (0, 1):
        field[Q + i, :own, :] = mid[len(FLAT) + i]
        field[Q + i, own:, :] = mid_e[len(FLAT) + i]
    total = None
    for t, c in tiles(rows, field.shape[2]):
        s = field[Q, t, c]
        out, rho, u, speed = collide([field[q, t, c] for q in range(Q)], s, field[Q + 1, t, c])
        for q in range(Q):
            post[q, t, c] = out[q]
        for i, value in enumerate([rho] + u + [speed]):
            field[Q + 2 + i, t, c] = value
        if t.start < own:
            e = (1.0 - s) * (rho * speed)
            total = e if total is None else total + e
    part[...] = total
    results = []
    for group in (FLAT, RISE, FALL):
        sums = [None, None, None]
        for q in group:
            cx, cy, _ = VEL[q]
            v = shifted(post[q], cx, cy)
            for k, sign in ((0, 1), (1, cx), (2, cy)):
                if sign:
                    if sums[k] is None:
                        sums[k] = v if sign > 0 else -v
                    else:
                        sums[k] = sums[k] + v if sign > 0 else sums[k] - v
        results.append(sums)
    for k in range(3):
        mom[k] = results[0][k]
        write_pair(odd, to_pair.at[k], to_other.at[k], results[1][k], results[2][k])


def kernel_three(odd_p, mom, pair, other, field, part, mine, to_pair, to_other, kinetic, out):
    rows = mom.shape[1]
    own = rows - 2 * HALO
    odd = odd_p[0] == 1
    total = part[...]
    for t, c in tiles(rows, field.shape[2]):
        below = [pick(odd, other[k, t, c], pair[k, t, c]) for k in range(3)]
        above = [pick(odd, pair[k, t, c], other[k, t, c]) for k in range(3)]
        rho = mom[0, t, c] + below[0] + above[0]
        inv = 1.0 / rho
        ux = (mom[1, t, c] + below[1] + above[1]) * inv
        uy = (mom[2, t, c] + below[2] + above[2]) * inv
        uz = (below[0] - above[0]) * inv
        speed = ux * ux + uy * uy + uz * uz
        free = 1.0 - field[Q, t, c]
        two = 2.0 * free
        ax, ay, az, b = two * ux, two * uy, two * uz, free * speed
        mine[0, t, c] = ax
        mine[1, t, c] = ay
        mine[2, t, c] = b
        to_pair[0, t, c] = ax
        to_pair[1, t, c] = ay
        to_other[0, t, c] = ax
        to_other[1, t, c] = ay
        write_pair(odd, to_pair.at[2, t, c], to_other.at[2, t, c], -az - b, az - b)
        if t.start < own:
            k = rho * speed
            kinetic[t, c] = k
            total = total + free * k
    out[...] = total


def fill_adjoint(lam, group, sources):
    for q in group:
        cx, cy, cz = VEL[q]
        ref = sources[cz]
        value = ref[2]
        if cz == 0:
            value = -value
        if cx:
            value = value + ref[0] if cx > 0 else value - ref[0]
        if cy:
            value = value + ref[1] if cy > 0 else value - ref[1]
        lam[q] = shifted(value, -cx, -cy)


def energy_part(q, out, two, less):
    e = out - less
    return e + dot_c(q, two) if q else e


def kernel_near(field, mine, energy, flat, near, shares, lam, adj, block, sems):
    for i in range(block.shape[0]):
        block[i] = energy[...]
    copy = pltpu.make_async_copy(block, shares, sems.at[0])
    copy.start()
    rows = field.shape[1]
    own = rows - 2 * HALO
    fill_adjoint(lam, FLAT, {0: mine})
    for t, c in tiles(rows, field.shape[2]):
        s, label = field[Q, t, c], field[Q + 1, t, c]
        rho, u, speed = stored(field, t, c)
        rate, keep, gain = rates(s, label)
        inlet = label == 3.0
        here = {q: jnp.where(inlet, 0.0, lam[q, t, c]) for q in FLAT}
        by_rho, by_mom, _ = by_moments(here, FLAT, u, speed)
        g0 = gain * by_rho
        gm = [gain * by_mom[a] for a in range(2)]
        near[0, t, c] = g0
        near[1, t, c] = gm[0]
        near[2, t, c] = gm[1]
        out = spread(here, FLAT, s, keep, g0, gm + [None])
        free = 1.0 - s
        two = [2.0 * free * u[a] for a in range(3)]
        less = free * speed
        for i, q in enumerate(FLAT):
            adj[i, t, c] = energy_part(q, out[q], two, less)
    for i, q in enumerate(FLAT):
        flat[i] = shifted(adj[i], -VEL[q][0], -VEL[q][1])[:own]
    copy.wait()


def kernel_four(odd_p, field, mine, pair, other, kinetic, near, late, to_pair, to_other, lam, adj):
    rows = field.shape[1]
    own = rows - 2 * HALO
    odd = odd_p[0] == 1
    low = [pick(odd, other[k], pair[k]) for k in range(3)]
    high = [pick(odd, pair[k], other[k]) for k in range(3)]
    fill_adjoint(lam, range(Q), {0: mine, 1: high, -1: low})
    for t, c in tiles(rows, field.shape[2]):
        s = field[Q, t, c]
        out, by_s, rho, u, speed, through = pull_back(
            [lam[q, t, c] for q in range(Q)],
            [field[q, t, c] for q in range(Q)],
            s,
            field[Q + 1, t, c],
            sorted(RISE + FALL),
            stored(field, t, c),
        )
        free = 1.0 - s
        two = [2.0 * free * u[a] for a in range(3)]
        less = free * speed
        for q in RISE + FALL:
            adj[q, t, c] = energy_part(q, out[q], two, less)
        for k in range(3):
            late[k, t, c] = through[k] - near[k, t, c]
        if t.start < own:
            late[3, t, c] = by_s - rho * speed - kinetic[t, c]
        else:
            late[3, t, c] = jnp.zeros_like(s)

    def pulled(q):
        return shifted(adj[q], -VEL[q][0], -VEL[q][1])[:own]

    for i in range(len(RISE)):
        write_pair(odd, to_pair.at[i], to_other.at[i], pulled(FALL[i]), pulled(RISE[i]))


def kernel_five(cells, odd_z, pop, cell, flat, late, pair, other, energy, sens_h, out_h, sens, out, level, sems):
    own = pop.shape[1]
    odd = odd_z[0] == 1
    copies = []
    for i, q in enumerate(FLAT):
        cx, cy, _ = VEL[q]
        value = late[0]
        if cx:
            value = value + late[1] if cx > 0 else value - late[1]
        if cy:
            value = value + late[2] if cy > 0 else value - late[2]
        level[i] = flat[i] + shifted(value, -cx, -cy)[:own]
    scale = cells / jnp.sum(jnp.sum(energy[...], axis=0), keepdims=True)
    scale = jnp.broadcast_to(scale, (8, pop.shape[2]))
    for t in bands(own):
        s, label = cell[0, t, :], cell[1, t, :]
        lam = []
        for q in range(Q):
            if VEL[q][2] == 0:
                lam.append(level[FLAT.index(q), t, :])
            elif VEL[q][2] == 1:
                i = RISE.index(q)
                lam.append(pick(odd, pair[i, t, :], other[i, t, :]))
            else:
                i = FALL.index(q)
                lam.append(pick(odd, other[i, t, :], pair[i, t, :]))
        grads, by_s, _, _, _, _ = pull_back(lam, [pop[q, t, :] for q in range(Q)], s, label, range(Q))
        for q in range(Q):
            out[q, t, :] = grads[q] * scale
        sens[t, :] = jnp.where(label == 1.0, (by_s + late[3, t, :]) * scale, 0.0)
        n = t.start // 8
        copies.append(pltpu.make_async_copy(out.at[:, t, :], out_h.at[:, t, :], sems.at[n]))
        copies[-1].start()
    copies.append(pltpu.make_async_copy(sens, sens_h, sems.at[own // 8]))
    copies[-1].start()
    for c in copies:
        c.wait()


def call(kernel, shapes, scratch, flags, *args, hbm_out=0, sems=0, aliases=None):
    fast = pl.BlockSpec(memory_space=pltpu.VMEM)
    slow = pl.BlockSpec(memory_space=pltpu.HBM)
    return pl.pallas_call(
        kernel,
        out_shape=[jax.ShapeDtypeStruct(s, jnp.float32) for s in shapes],
        in_specs=[pl.BlockSpec(memory_space=pltpu.SMEM)] * len(flags)
        + [fast] * len(args),
        out_specs=[fast] * (len(shapes) - hbm_out) + [slow] * hbm_out,
        scratch_shapes=[pltpu.VMEM(s, jnp.float32) for s in scratch]
        + ([pltpu.SemaphoreType.DMA((sems,))] if sems else []),
        input_output_aliases=aliases or {},
        compiler_params=pltpu.CompilerParams(vmem_limit_bytes=16 * 1024 * 1024),
    )(*flags, *args)


class Layout:
    def __init__(self, planes, chunks):
        self.planes, self.chunks = planes, chunks
        self.bricks = [(p, k) for p in range(planes) for k in range(chunks)]
        self.swapped = planes % 2 == 0 and chunks % 2 == 0

    def start(self, p, k):
        return (p % self.planes) * self.chunks + k % self.chunks

    def home(self, p, k):
        p, k = p % self.planes, k % self.chunks
        if not self.swapped:
            return self.start(p, k)
        return self.start(p - p % 2 + (k + ALPHA) % 2, k - k % 2 + (p + BETA) % 2)

    def moves(self, source, target):
        side = lambda p: 1 - 2 * (p % 2)
        still = [(source(p, k), target(p, k)) for p, k in self.bricks]
        pair = [(source(p, k), target(p + side(p), k)) for p, k in self.bricks]
        other = [(source(p, k), target(p - side(p), k)) for p, k in self.bricks]
        return still, pair, other


def on_device(populations, solid_fraction, labels):
    _, _, own, wide = populations.shape
    rows = own + 2 * HALO
    axes = ("gz", "gy")
    planes, chunks = lax.axis_size("gz"), lax.axis_size("gy")
    layout = Layout(planes, chunks)
    flag = lambda axis: (lax.axis_index(axis) % 2).astype(jnp.int32).reshape(1)
    odd_z, odd_y = flag("gz"), flag("gy")
    odd_p = (odd_y + BETA) % 2 if layout.swapped else odd_z
    pop = populations.reshape(Q, own, wide)
    frac = solid_fraction.reshape(own, wide)
    lab = labels.reshape(own, wide)
    whole = lambda n: (n, rows, wide)
    less = lambda n: (n, own, wide)
    edge = lambda n: (n, 2 * HALO, wide)

    marks = lax.optimization_barrier(lab.astype(jnp.float32))
    mixed = jnp.where(marks == 1.0, frac, jnp.where(marks == 2.0, jnp.float32(1.0), jnp.float32(0.0)))
    cell = jnp.stack([mixed, marks])
    size = edge_slots(True)[1]
    edge_a, edge_b, mid, pair, other = call(
        kernel_one,
        [(size, wide)] * 2 + [less(11), whole(5), whole(5)],
        [less(Q)],
        [odd_z, odd_y],
        pop,
        cell,
    )
    side = lambda k: 1 - 2 * (k % 2)
    edge_a = lax.ppermute(edge_a, "gy", [(k, (k + side(k)) % chunks) for k in range(chunks)])
    edge_b = lax.ppermute(edge_b, "gy", [(k, (k - side(k)) % chunks) for k in range(chunks)])
    still_p, pair_p, other_p = layout.moves(layout.start, layout.home)
    mid = lax.ppermute(mid, axes, still_p)
    mid_e, pair, other = call(
        kernel_edge,
        [edge(11), whole(5), whole(5)],
        [],
        [odd_z, odd_y],
        edge_a,
        edge_b,
        pair,
        other,
        aliases={4: 1, 5: 2},
    )
    mid_e = lax.ppermute(mid_e, axes, still_p)
    other = lax.ppermute(other, axes, other_p)
    pair = lax.ppermute(pair, axes, pair_p)
    field, mom, pair, other, part = call(
        kernel_two,
        [whole(Q + 7), whole(3), whole(3), whole(3), (8, wide // 2)],
        [(rows, wide), whole(Q)],
        [odd_p],
        mid,
        pair,
        other,
        mid_e,
    )
    _, pair_p, other_p = layout.moves(layout.home, layout.home)
    other = lax.ppermute(other, axes, other_p)
    pair = lax.ppermute(pair, axes, pair_p)
    mine, pair, other, kinetic, energy = call(
        kernel_three,
        [whole(3), whole(3), whole(3), (own, wide), (8, wide // 2)],
        [],
        [odd_p],
        mom,
        pair,
        other,
        field,
        part,
    )
    other = lax.ppermute(other, axes, other_p)
    pair = lax.ppermute(pair, axes, pair_p)
    count = planes * chunks
    flat, near, energy = call(
        kernel_near,
        [less(9), whole(3), (count, 8, wide // 2)],
        [whole(Q), whole(9), (count, 8, wide // 2)],
        [],
        field,
        mine,
        energy,
        hbm_out=1,
        sems=1,
    )
    energy = lax.all_to_all(energy, axes, 0, 0, tiled=True)
    late, pair, other = call(
        kernel_four,
        [whole(4), less(5), less(5)],
        [whole(Q), whole(Q)],
        [odd_p],
        field,
        mine,
        pair,
        other,
        kinetic,
        near,
    )
    still_p, pair_p, other_p = layout.moves(layout.home, layout.start)
    flat = lax.ppermute(flat, axes, still_p)
    pair = lax.ppermute(pair, axes, pair_p)
    other = lax.ppermute(other, axes, other_p)
    late = lax.ppermute(late, axes, still_p)
    cells = float(STEPS * own * wide * populations.shape[1] * planes * chunks)
    sens, out = call(
        functools.partial(kernel_five, cells),
        [(own, wide), less(Q)],
        [(own, wide), less(Q), less(9)],
        [odd_z],
        pop,
        cell,
        flat,
        late,
        pair,
        other,
        energy,
        hbm_out=2,
        sems=own // 8 + 1,
    )
    return sens.reshape(solid_fraction.shape), out.reshape(populations.shape)


def solution(mesh):
    in_specs = (P(None, "gz", "gy", None), P("gz", "gy", None), P("gz", "gy", None))
    out_specs = (P("gz", "gy", None), P(None, "gz", "gy", None))
    return jax.shard_map(on_device, mesh=mesh, in_specs=in_specs, out_specs=out_specs, check_vma=False)
```
